128 devices in a mesh: member: 8 (over x, core), mp: 16 (over y, z).
Axes of the slice: x: 4, y: 4, z: 4, core: 2. Of those that a mesh axis runs over, the one named last changes fastest.
Arguments:
- hidden: bfloat16 [8, 2048, 1024], P('member', 'mp'), may hold values from -6 to 6
- grid_emb: bfloat16 [8, 16384, 1024], P('member', 'mp'), may hold values from -6 to 6
- targets: float32 [100, 16384], P(None, 'mp'), may hold values from -6 to 6
- area_w: float32 [16384], P('mp'), may hold values from 1 to 10
- field_w: float32 [100], replicated, may hold values from 0.3 to 3
- edge_table: int32 [16384, 3], P('mp'), may hold values from 0 to 255, as said below
- halo_rows: int32 [64, 32], P('mp'), may hold values from 0 to 127, as said below
- w_query: bfloat16 [1024, 1024], replicated, may hold values from -0.1875 to 0.1875
- w_keyval: bfloat16 [2048, 1024], replicated, may hold values from -0.1875 to 0.1875
- w_attn_out: bfloat16 [1024, 1024], replicated, may hold values from -0.1875 to 0.1875
- w_fields: bfloat16 [100, 1024], replicated, may hold values from -0.1875 to 0.1875
Outputs:
- d_hidden: bfloat16 [8, 2048, 1024], P('member', 'mp')
- d_grid: bfloat16 [8, 16384, 1024], P('member', 'mp')
- grad_wq: float32 [1024, 1024], P(('member', 'mp'))
- grad_wkv: float32 [2048, 1024], P(('member', 'mp'))
- grad_wo: float32 [1024, 1024], P(('member', 'mp'))
- grad_wf: float32 [100, 1024], replicated
The draws below stay inside these ranges and needn't reach their ends.
Inputs may be any that keep to these rules, and one draw needn't show every extreme that they name: `halo_rows`: the four rows of device d's block list the local hidden nodes (row numbers within d's 128) that d sends to the mp devices at offsets -2, -1, +1, +2 (cyclic), in that order. Each list holds distinct rows in its first L entries, L from 16 to 32, with L = 32 for some list, and zeros after them. `edge_table`: entries index a table of 256 rows on the point's device: below 128 the device's own hidden nodes; 128 + r * 32 + p is entry p of the list that the device at offset -2, -1, +1, +2 (r = 0 to 3) sends to this device, with p below that list's filled length.
All inputs are finite; a program needn't handle non-finite values.
Results may differ from the reference program's by a relative error of at most 0.035.
Values may be sent and summed in bfloat16 or wider, within the bound.
A program may use at most 192 MiB of HBM per device.

```python
import math
import jax
import jax.numpy as jnp
from jax import lax

C = 1024
HEADS = 16
F = 100
K = 3
G_DEV = 1024
NH_DEV = 128
HALO = 32
MEMBERS = 8
GRID = 16384
HIDDEN_SIZE = 2048
SLOTS = 64


OFFSETS = (-2, -1, 1, 2)


def fullest_slot(key):
    return (4 * jax.random.randint(jax.random.fold_in(key, 99), (), 0, SLOTS // 4)).astype(jnp.int32)


def list_lengths(key):
    lengths = jax.random.randint(key, (SLOTS,), HALO // 2, HALO + 1)
    return lengths.at[fullest_slot(key)].set(HALO).astype(jnp.int32)


def draw_halo_rows(key, part):
    lengths = list_lengths(key)
    key = jax.random.fold_in(key, 3)
    keys = jax.random.split(key, SLOTS)
    orders = jax.vmap(lambda subkey: jax.random.permutation(subkey, NH_DEV)[:HALO])(keys)
    positions = jnp.arange(HALO, dtype=jnp.int32)[None, :]
    return jnp.where(positions < lengths[:, None], orders, 0).astype(jnp.int32)


def draw_edge_table(key, part):
    lengths = list_lengths(key)
    fullest = fullest_slot(key)
    key = jax.random.fold_in(key, 5)
    devices_mp = SLOTS // 4
    owner = jnp.arange(GRID, dtype=jnp.int32) // G_DEV
    keys = jax.random.split(key, 7)

    def remote(key_first, key_second):
        which = jax.random.randint(key_first, (GRID,), 0, 4)
        shifts = jnp.array(OFFSETS, dtype=jnp.int32)[which]
        source = (owner + shifts) % devices_mp
        length = lengths[source * 4 + 3 - which]
        position = jax.random.randint(key_second, (GRID,), 0, 1 << 20) % length
        return NH_DEV + which * HALO + position
    first = jax.random.randint(keys[0], (GRID,), 0, NH_DEV)
    second = remote(keys[1], keys[2])
    third_local = jax.random.randint(keys[3], (GRID,), 0, NH_DEV)
    coin = jax.random.randint(keys[4], (GRID,), 0, 2)
    third = jnp.where(coin == 0, third_local, remote(keys[5], jax.random.fold_in(keys[5], 1)))
    receiver = (fullest // 4 - 2) % devices_mp
    chosen = receiver * G_DEV + jax.random.randint(keys[6], (), 0, G_DEV)
    second = second.at[chosen].set(NH_DEV + 4 * HALO - 1)
    return jnp.stack([first, second, third], axis=1).astype(jnp.int32)


def shard_levels(rng, dims, cuts, low, largest):
    loudness, own = 1.0, jax.random.fold_in(rng, 6)
    for axis_at, parts in cuts:
        steps = jnp.exp(jax.random.uniform(jax.random.fold_in(own, axis_at), (parts,), jnp.float32, low / len(cuts), largest / len(cuts)))
        loudness = loudness * jnp.repeat(steps, dims[axis_at] // parts).reshape([-1 if axis == axis_at else 1 for axis in range(len(dims))])
    return loudness


def bell_draw(stream_key, extent, width, most, pieces=(), held_as=jnp.bfloat16):
    entries = width * jax.random.normal(stream_key, extent, jnp.float32)
    if pieces:
        entries = entries * shard_levels(stream_key, extent, pieces, -0.22, 0.18)
    return jnp.clip(entries, -most, most).astype(held_as)


def setup_inputs(seed: int = 0) -> dict:
    key_list = jax.random.split(jax.random.key(seed), 12)
    hidden = bell_draw(key_list[0], (MEMBERS, HIDDEN_SIZE, C), 1.0, 6.0, ((0, 8), (1, 16)))
    grid_emb = bell_draw(key_list[1], (MEMBERS, GRID, C), 1.0, 6.0, ((0, 8), (1, 16)))
    targets = bell_draw(key_list[2], (F, GRID), 1.0, 6.0, ((1, 16),), jnp.float32)
    area_w = jnp.clip(jnp.exp(math.log(10.0) - 2.3025851 * jax.random.uniform(key_list[3], (GRID,), jnp.float32) ** shard_levels(key_list[3], (GRID,), ((0, 16),), -0.2, 0.2)), 1.0, 10.0)
    field_w = jnp.clip(jnp.exp(jax.random.uniform(key_list[4], (F,), jnp.float32, math.log(0.3), math.log(3.0))), 0.3, 3.0)
    edge_table = draw_edge_table(jax.random.fold_in(key_list[11], 71), 0)
    halo_rows = draw_halo_rows(jax.random.fold_in(key_list[11], 71), 0)
    w_query = bell_draw(key_list[7], (C, C), C ** -0.5, 0.1875)
    w_keyval = bell_draw(key_list[8], (2 * C, C), C ** -0.5, 0.1875)
    w_attn_out = bell_draw(key_list[9], (C, C), C ** -0.5, 0.1875)
    w_fields = bell_draw(key_list[10], (F, C), C ** -0.5, 0.1875)
    return {"hidden": hidden, "grid_emb": grid_emb, "targets": targets, "area_w": area_w, "field_w": field_w, "edge_table": edge_table, "halo_rows": halo_rows, "w_query": w_query, "w_keyval": w_keyval, "w_attn_out": w_attn_out, "w_fields": w_fields}


ALPHA_FAIR = 0.95
KAPPA = 0.1
OFFSETS = (-2, -1, 1, 2)

def soft_sign(value):
    return value / jnp.sqrt(value * value + KAPPA * KAPPA)

def global_sources(edge_table, halo_rows):
    devices_mp = SLOTS // 4
    owner = (jnp.arange(GRID, dtype=jnp.int32) // G_DEV)[:, None]
    beyond = jnp.maximum(edge_table - NH_DEV, 0)
    which = beyond // HALO
    position = beyond % HALO
    shifts = jnp.array(OFFSETS, dtype=jnp.int32)[which]
    source = (owner + shifts) % devices_mp
    listed = halo_rows[(source * 4 + 3 - which).astype(jnp.int32), position.astype(jnp.int32)]
    remote = source * NH_DEV + listed
    local = owner * NH_DEV + edge_table
    return jnp.where(edge_table < NH_DEV, local, remote).astype(jnp.int32)

def forward(hidden_one, grid_one, sources, weights_all):
    w_query, w_keyval, w_attn_out, w_fields = weights_all
    head_dim = C // HEADS
    root = math.sqrt(head_dim)
    query = lax.optimization_barrier(jnp.dot(grid_one, w_query.T, preferred_element_type=jnp.float32).astype(jnp.bfloat16))
    keyval = lax.optimization_barrier(jnp.dot(hidden_one, w_keyval.T, preferred_element_type=jnp.float32).astype(jnp.bfloat16))
    picked = keyval[sources].astype(jnp.float32)
    keys = picked[:, :, :C].reshape(GRID, K, HEADS, head_dim)
    values = picked[:, :, C:].reshape(GRID, K, HEADS, head_dim)
    query_heads = query.astype(jnp.float32).reshape(GRID, HEADS, head_dim)
    scores = jnp.einsum('ghd,gkhd->gkh', query_heads, keys) / root
    raised = jnp.exp(scores)
    weights = raised / lax.optimization_barrier(jnp.sum(raised, axis=1, keepdims=True))
    rounded = lax.optimization_barrier(weights.astype(jnp.bfloat16)).astype(jnp.float32)
    attended = jnp.einsum('gkh,gkhd->ghd', rounded, values).reshape(GRID, C).astype(jnp.bfloat16)
    mixed = (grid_one.astype(jnp.float32) + jnp.dot(attended, w_attn_out.T, preferred_element_type=jnp.float32)).astype(jnp.bfloat16)
    predicted = jnp.dot(w_fields, mixed.T, preferred_element_type=jnp.float32)
    return (predicted, (query_heads, keys, values, weights, rounded, attended, mixed))

def backward(hidden_one, grid_one, d_pred_one, sources, weights_all):
    w_query, w_keyval, w_attn_out, w_fields = weights_all
    head_dim = C // HEADS
    root = math.sqrt(head_dim)
    predicted, saved = forward(hidden_one, grid_one, sources, weights_all)
    query_heads, keys, values, weights, rounded, attended, mixed = saved
    d_mixed = jnp.dot(d_pred_one.T, w_fields, preferred_element_type=jnp.float32).astype(jnp.bfloat16)
    grad_fields = jnp.dot(d_pred_one, mixed, preferred_element_type=jnp.float32)
    d_attended = jnp.dot(d_mixed, w_attn_out, preferred_element_type=jnp.float32).reshape(GRID, HEADS, head_dim)
    grad_out = jnp.dot(d_mixed.T, attended, preferred_element_type=jnp.float32)
    d_values = rounded[..., None] * d_attended[:, None]
    d_weights = jnp.einsum('ghd,gkhd->gkh', d_attended, values)
    d_scores = weights * (d_weights - lax.optimization_barrier(jnp.sum(weights * d_weights, axis=1, keepdims=True)))
    d_query = (jnp.einsum('gkh,gkhd->ghd', d_scores, keys) / root).reshape(GRID, C).astype(jnp.bfloat16)
    d_keys = d_scores[..., None] * query_heads[:, None] / root
    d_pairs = jnp.concatenate([d_keys.reshape(GRID, K, C), d_values.reshape(GRID, K, C)], axis=2)
    d_keyval = jax.ops.segment_sum(d_pairs.reshape(GRID * K, 2 * C), sources.reshape(-1), num_segments=HIDDEN_SIZE).astype(jnp.bfloat16)
    d_hidden = jnp.dot(d_keyval, w_keyval, preferred_element_type=jnp.float32).astype(jnp.bfloat16)
    grad_keyval = jnp.dot(d_keyval.T, hidden_one, preferred_element_type=jnp.float32)
    d_grid = (d_mixed.astype(jnp.float32) + jnp.dot(d_query, w_query, preferred_element_type=jnp.float32)).astype(jnp.bfloat16)
    grad_query = jnp.dot(d_query.T, grid_one, preferred_element_type=jnp.float32)
    return (d_hidden, d_grid, grad_query, grad_keyval, grad_out, grad_fields)

def reference(hidden, grid_emb, targets, area_w, field_w, edge_table, halo_rows, w_query, w_keyval, w_attn_out, w_fields):
    sources = global_sources(edge_table, halo_rows)
    weights_all = (w_query, w_keyval, w_attn_out, w_fields)

    def predict(member):
        return forward(member[0], member[1], sources, weights_all)[0]
    predicted = lax.map(predict, (hidden, grid_emb))
    scale = field_w[:, None] * area_w[None, :]
    fair = (1.0 - (1.0 - ALPHA_FAIR) / MEMBERS) / (MEMBERS * (MEMBERS - 1))
    spread = jnp.zeros_like(predicted)
    for other in range(MEMBERS):
        spread = spread + soft_sign(predicted - predicted[other][None])
    d_pred = (scale * (soft_sign(predicted - targets[None]) / MEMBERS - fair * spread)).astype(jnp.bfloat16)

    def differentiate(member):
        return backward(member[0], member[1], member[2], sources, weights_all)
    d_hidden, d_grid, grad_q, grad_kv, grad_o, grad_f = lax.map(differentiate, (hidden, grid_emb, d_pred))
    norm = 1.0 / math.sqrt(MEMBERS * GRID)
    return (d_hidden, d_grid, lax.optimization_barrier(jnp.sum(grad_q, axis=0)) * norm, lax.optimization_barrier(jnp.sum(grad_kv, axis=0)) * norm, lax.optimization_barrier(jnp.sum(grad_o, axis=0)) * norm, lax.optimization_barrier(jnp.sum(grad_f, axis=0)) * norm)
```

```python
import functools
import math

import jax
import jax.numpy as jnp
from jax import lax
from jax.experimental import pallas as pl
from jax.experimental.pallas import tpu as pltpu
from jax.sharding import PartitionSpec as P

HEADS = 16
HEAD_DIM = 64
ALPHA_FAIR = 0.95
KAPPA = 0.1
OFFSETS = (-2, -1, 1, 2)
MEMBERS = 8
FIELD_ROWS = 112
LANES = 256
MESH = pl.DeviceIdType.MESH
BF16 = jnp.bfloat16
F32 = jnp.float32
NT = (((1,), (1,)), ((), ()))
NN = (((1,), (0,)), ((), ()))


def dot(left, right, numbers=NN):
    return lax.dot_general(left, right, numbers, preferred_element_type=F32)


def soft_sign(value):
    return value * lax.rsqrt(value * value + KAPPA * KAPPA)


def blocks(count, body):
    def step(at, carry):
        body(at)
        return carry

    lax.fori_loop(0, count, step, 0)


def kernel(
    hid_hbm, grid_hbm, tgt_ref, area_ref, field_ref, edge_ref, halo_ref,
    wq_hbm, wkv_hbm, wo_hbm, wf_ref,
    dhid_ref, dgrid_hbm, gq_ref, gkv_ref, go_ref, gf_ref,
    grid_v, wq_v, wkv_v, wo_v, wot_v, tgrid, qt, att, mix, th, tkv, oht, kvg, wts,
    wfp, wft, tpad, preds, predr, dps, dpr, dpf,
    datt, dkv_last, outgo, drecv,
    fs, fr1, fr2, fr3, fr4,
    send_buf, recv_buf,
    w_own, w_r1, w_s1, w_r2, w_fin,
    h_own, h_r1, h_s1, h_r2, h_fin,
    rx,
    load_sem, halo_s, halo_r, ps_s, ps_r, dp_s, dp_r, back_s, back_r,
    f1_s, f1_r, f2_s, f2_r, f3_s, f3_r, f4_s, f4_r,
    core_s, core_r, one_s, one_r, two_s, two_r, x_s, x_r, out_sem,
):
    me = lax.axis_index("member")
    mp = lax.axis_index("mp")
    x, c = lax.div(me, 2), lax.rem(me, 2)
    y, z = lax.div(mp, 4), lax.rem(mp, 4)
    other = 1 - c
    sibling = (2 * x + other, mp)
    norm = 1.0 / math.sqrt(MEMBERS * 16384.0)

    def halo_peer(by):
        return (me, lax.rem(mp + by + 16, 16))

    def member_peer(by):
        return lax.rem(me + by, 8)

    def y_peer(by):
        return (me, 4 * lax.rem(y + by, 4) + z)

    def z_peer(by):
        return (me, 4 * y + lax.rem(z + by, 4))

    def remote(src, dst, send, recv, device):
        return pltpu.make_async_remote_copy(
            src_ref=src, dst_ref=dst, send_sem=send, recv_sem=recv,
            device_id=device, device_id_type=MESH,
        )

    loads = [
        pltpu.make_async_copy(src, dst, load_sem.at[n])
        for n, (src, dst) in enumerate((
            (hid_hbm, th.at[pl.ds(0, 128)]), (grid_hbm, grid_v), (wq_hbm, wq_v),
            (wkv_hbm, wkv_v), (wo_hbm, wo_v),
        ))
    ]
    for load in loads:
        load.start()
    barrier = pltpu.get_barrier_semaphore()
    partners = (
        [halo_peer(by) for by in OFFSETS]
        + [(member_peer(by), mp) for by in range(1, 8)]
        + [y_peer(by) for by in range(1, 4)]
        + [z_peer(by) for by in range(1, 4)]
    )
    for partner in partners:
        pl.semaphore_signal(barrier, inc=1, device_id=partner, device_id_type=MESH)

    halo_hot = (
        halo_ref[...] == lax.broadcasted_iota(jnp.int32, (128, 128), 1)
    ).astype(BF16)
    loads[0].wait()
    outgo[...] = dot(halo_hot, th[pl.ds(0, 128), :]).astype(BF16)
    pl.semaphore_wait(barrier, len(partners))
    halos = []
    for l, by in enumerate(OFFSETS):
        copy = remote(
            outgo.at[pl.ds(32 * l, 32)], th.at[pl.ds(128 + 32 * (3 - l), 32)],
            halo_s.at[l], halo_r.at[3 - l], halo_peer(by),
        )
        copy.start()
        halos.append(copy)

    for e in range(3):
        def hot(at, e=e):
            rows = pl.ds(pl.multiple_of(at * 256, 256), 256)
            oht[e, rows, :] = (
                edge_ref[rows, e:e + 1] == lax.broadcasted_iota(jnp.int32, (256, 256), 1)
            ).astype(BF16)
        blocks(4, hot)
    wfp[...] = jnp.zeros_like(wfp)
    wfp[pl.ds(0, 100), :] = wf_ref[...]
    wft[...] = wfp[...].T
    tpad[...] = jnp.zeros_like(tpad)
    tpad[pl.ds(0, 100), :] = tgt_ref[:, pl.ds(pl.multiple_of(me * 128, 128), 128)]
    dpf[...] = jnp.zeros_like(dpf)

    loads[1].wait()

    def turn(at):
        span = pl.ds(pl.multiple_of(at * 256, 256), 256)
        tgrid[:, span] = grid_v[span, :].T
    blocks(4, turn)
    loads[2].wait()

    def make_query(at):
        span = pl.ds(pl.multiple_of(at * 256, 256), 256)
        qt[:, span] = dot(wq_v[...], tgrid[:, span]).astype(BF16)
    blocks(4, make_query)

    loads[3].wait()
    for copy in halos:
        copy.wait()

    def make_table(at):
        span = pl.ds(pl.multiple_of(at * 512, 512), 512)
        tkv[span, :] = dot(wkv_v[span, :], th[...], NT).astype(BF16)
    blocks(4, make_table)
    for e in range(3):
        def gather(at, e=e):
            span = pl.ds(pl.multiple_of(at * 512, 512), 512)
            kvg[e, span, :] = dot(tkv[span, :], oht[e], NT).astype(BF16)
        blocks(4, gather)
    loads[4].wait()

    def send_pred(target):
        return remote(
            preds.at[target], predr.at[me], ps_s.at[target], ps_r.at[me], (target, mp)
        )

    def tile(at):
        lanes = pl.ds(pl.multiple_of(at * LANES, LANES), LANES)

        def head(h):
            rows = pl.ds(pl.multiple_of(h * 64, 64), 64)
            vrows = pl.ds(pl.multiple_of(1024 + h * 64, 64), 64)
            query = qt[rows, lanes].astype(F32)
            raised = []
            for e in range(3):
                key = kvg[e, rows, lanes].astype(F32)
                raised.append(jnp.exp(jnp.sum(query * key, axis=0, keepdims=True) * 0.125))
            total = raised[0] + raised[1] + raised[2]
            out = None
            for e in range(3):
                weight = raised[e] / total
                wts[h, e:e + 1, lanes] = weight
                term = weight.astype(BF16).astype(F32) * kvg[e, vrows, lanes].astype(F32)
                out = term if out is None else out + term
            att[rows, lanes] = out.astype(BF16)
        blocks(16, head)
        mixed = (tgrid[:, lanes].astype(F32) + dot(wo_v[...], att[:, lanes])).astype(BF16)
        mix[:, lanes] = mixed
        pred = dot(wfp[pl.ds(0, FIELD_ROWS), :], mixed)
        for half in range(2):
            target = 2 * at + half
            preds[target] = pred[:, 128 * half:128 * half + 128]

            @pl.when(target != me)
            def _():
                send_pred(target).start()

            @pl.when(target == me)
            def _():
                predr[me] = pred[:, 128 * half:128 * half + 128]
    blocks(4, tile)

    def turn_out(at):
        span = pl.ds(pl.multiple_of(at * 256, 256), 256)
        wot_v[:, span] = wo_v[span, :].T
    blocks(4, turn_out)

    for by in range(1, 8):
        source = member_peer(by)
        remote(preds.at[source], predr.at[source], ps_s.at[source], ps_r.at[source],
               (source, mp)).wait()
    fair = (1.0 - (1.0 - ALPHA_FAIR) / MEMBERS) / (MEMBERS * (MEMBERS - 1))
    area = area_ref[:, pl.ds(pl.multiple_of(me * 128, 128), 128)]

    def crps(at):
        rows = pl.ds(pl.multiple_of(at * 16, 16), 16)
        truth = tpad[rows, :]
        scale = field_ref[rows, :] * area
        pred = [predr[m, rows, :] for m in range(MEMBERS)]
        spread = [jnp.zeros((16, 128), F32) for _ in range(MEMBERS)]
        for i in range(MEMBERS):
            for j in range(i + 1, MEMBERS):
                term = soft_sign(pred[i] - pred[j])
                spread[i] = spread[i] + term
                spread[j] = spread[j] - term
        for m in range(MEMBERS):
            dps[m, rows, :] = (
                scale * (soft_sign(pred[m] - truth) * (1.0 / MEMBERS) - fair * spread[m])
            ).astype(BF16)
    blocks(FIELD_ROWS // 16, crps)
    d_copies = []
    for by in range(1, 8):
        target = member_peer(by)
        copy = remote(dps.at[target], dpr.at[me], dp_s.at[by], dp_r.at[me], (target, mp))
        copy.start()
        d_copies.append(copy)
    dpr[me] = dps[me]
    for by in range(1, 8):
        source = member_peer(by)
        remote(dps.at[source], dpr.at[source], dp_s.at[by], dp_r.at[source],
               (source, mp)).wait_recv()
    for copy in d_copies:
        copy.wait_send()
    for j in range(MEMBERS):
        dpf[pl.ds(0, FIELD_ROWS), 128 * j:128 * j + 128] = dpr[j]

    dmix = tgrid

    def make_dmix(at):
        span = pl.ds(pl.multiple_of(at * 256, 256), 256)
        dmix[span, :] = dot(wft[span, :], dpf[...]).astype(BF16)
    blocks(4, make_dmix)

    def halves(half, peer):
        return y_peer(peer) if half == 0 else z_peer(peer)

    def store_unit(ref, unit, value, paired):
        if paired:
            value = value.reshape(2, 16, 8, 512).transpose(1, 0, 2, 3).reshape(256, 512)
        ref[0, unit] = value[:, :256].astype(BF16)
        second = value[:, 256:].reshape(4, 4, 16, 256).transpose(1, 0, 2, 3).reshape(256, 256)
        ref[1, unit] = second.astype(BF16)

    units = [4, 3, 3, 3, 3]
    sets = [(send_buf, recv_buf.at[0], w_own, w_r1, w_s1, w_r2, w_fin)] + [
        (send_buf.at[:, pl.ds(0, 3)], recv_buf.at[n % 2, :, pl.ds(0, 3)])
        + tuple(ref.at[n - 1] for ref in (h_own, h_r1, h_s1, h_r2, h_fin))
        for n in range(1, 5)
    ]

    def core_copy(n):
        return remote(sets[n][0], sets[n][1], core_s.at[n], core_r.at[n], sibling)

    def one_copy(n, half, by):
        first = lax.rem((y if half == 0 else z) + by, 4)
        return remote(
            sets[n][2].at[half, :, pl.ds(pl.multiple_of(first * 64, 64), 64), :],
            sets[n][3].at[half, by - 1],
            one_s.at[n, half, by - 1], one_r.at[n, half, by - 1], halves(half, by),
        )

    def two_copy(n, half, by):
        second = lax.rem((z if half == 0 else y) + by, 4)
        return remote(
            sets[n][4].at[half, :, pl.ds(pl.multiple_of(second * 16, 16), 16), :],
            sets[n][5].at[half, by - 1],
            two_s.at[n, half, by - 1], two_r.at[n, half, by - 1], halves(1 - half, by),
        )

    def start_one(n):
        core_copy(n).wait()
        own, recv = sets[n][2], sets[n][1]
        for half in range(2):
            def add(unit, half=half):
                own[half, unit] = (
                    own[half, unit].astype(F32) + recv[half, unit].astype(F32)
                ).astype(BF16)
            blocks(units[n], add)
            for by in (2, 1, 3):
                one_copy(n, half, by).start()

    def start_two(n):
        for half in range(2):
            for by in (1, 3, 2):
                one_copy(n, half, by).wait()
            first = pl.ds(pl.multiple_of((y if half == 0 else z) * 64, 64), 64)
            own, r1, s1 = sets[n][2], sets[n][3], sets[n][4]
            for unit in range(units[n]):
                total = own[half, unit, first, :].astype(F32)
                for slot in range(3):
                    total = total + r1[half, slot, unit].astype(F32)
                s1[half, unit] = total.astype(BF16)
            for by in (2, 1, 3):
                two_copy(n, half, by).start()

    def x_targets(n):
        if n == 0:
            return [(0, i, 2 * i + k) for i in range(4) for k in range(2)]
        j = lax.rem(x + n, 4)
        return [(1, 0, 2 * j), (1, 0, 2 * j + 1), (2, 1, j), (2, 2, 4 + j)]

    def x_copy(n, index, kind, unit, target):
        return remote(
            sets[n][6].at[unit], rx.at[kind, me], x_s.at[n, index], x_r.at[kind, me],
            (target, mp),
        )

    def start_x(n):
        fin, s1, r2 = sets[n][6], sets[n][4], sets[n][5]
        for half in range(2):
            for by in (1, 3, 2):
                two_copy(n, half, by).wait()
            second = pl.ds(pl.multiple_of((z if half == 0 else y) * 16, 16), 16)
            for unit in range(units[n]):
                total = s1[half, unit, second, :].astype(F32)
                for slot in range(3):
                    total = total + r2[half, slot, unit].astype(F32)
                fin[unit, :, 256 * half:256 * half + 256] = total.astype(BF16)
        for index, (kind, unit, target) in enumerate(x_targets(n)):
            @pl.when(target != me)
            def _():
                x_copy(n, index, kind, unit, target).start()

            @pl.when(target == me)
            def _():
                rx[kind, me] = fin[unit]

    def end_x(n):
        for index, (kind, unit, target) in enumerate(x_targets(n)):
            @pl.when(target != me)
            def _():
                x_copy(n, index, kind, unit, target).wait_send()

    own_cols = pl.ds(pl.multiple_of(c * 512, 512), 512)
    other_cols = pl.ds(pl.multiple_of(other * 512, 512), 512)

    for target_ref, cols in ((send_buf, other_cols), (w_own, own_cols)):
        def out_unit(unit):
            span = pl.ds(pl.multiple_of(unit * 256, 256), 256)
            store_unit(target_ref, unit, dot(dmix[span, :], att[cols, :], NT), True)
        blocks(4, out_unit)
        if target_ref is send_buf:
            core_copy(0).start()

    g_fields = dot(dpf[pl.ds(0, FIELD_ROWS), :], mix[...], NT)
    for j in range(MEMBERS):
        fs[j] = g_fields[:, 128 * j:128 * j + 128].astype(BF16)

    def f1_copy(by):
        target = member_peer(by)
        return remote(fs.at[target], fr1.at[me], f1_s.at[by], f1_r.at[me], (target, mp))

    for by in range(1, 8):
        f1_copy(by).start()
    fr1[me] = fs[me]
    start_one(0)

    def f2_copy(by):
        return remote(fr2.at[y], fr2.at[y], f2_s.at[by], f2_r.at[y], y_peer(by))

    def f3_copy(by):
        return remote(fr3.at[z], fr3.at[z], f3_s.at[by], f3_r.at[z], z_peer(by))

    def f4_copy(by):
        return remote(fr4.at[me], fr4.at[me], f4_s.at[by], f4_r.at[me], (member_peer(by), mp))

    def slots_sum(ref, count):
        total = ref[0].astype(F32)
        for slot in range(1, count):
            total = total + ref[slot].astype(F32)
        return total

    def start_f2():
        for by in range(1, 8):
            source = member_peer(by)
            remote(fs.at[source], fr1.at[source], f1_s.at[by], f1_r.at[source],
                   (source, mp)).wait_recv()
            f1_copy(by).wait_send()
        fr2[y] = slots_sum(fr1, 8).astype(BF16)
        for by in range(1, 4):
            f2_copy(by).start()

    def start_f3():
        for by in range(1, 4):
            source = lax.rem(y + by, 4)
            remote(fr2.at[source], fr2.at[source], f2_s.at[by], f2_r.at[source],
                   y_peer(by)).wait_recv()
            f2_copy(by).wait_send()
        fr3[z] = slots_sum(fr2, 4).astype(BF16)
        for by in range(1, 4):
            f3_copy(by).start()

    def start_f4():
        for by in range(1, 4):
            source = lax.rem(z + by, 4)
            remote(fr3.at[source], fr3.at[source], f3_s.at[by], f3_r.at[source],
                   z_peer(by)).wait_recv()
            f3_copy(by).wait_send()
        fr4[me] = (slots_sum(fr3, 4) * norm).astype(BF16)
        for by in range(1, 8):
            f4_copy(by).start()

    def end_f4():
        for by in range(1, 8):
            source = member_peer(by)
            remote(fr4.at[source], fr4.at[source], f4_s.at[by], f4_r.at[source],
                   (source, mp)).wait_recv()
            f4_copy(by).wait_send()
        for j in range(MEMBERS):
            gf_ref[:, 128 * j:128 * j + 128] = fr4[j, pl.ds(0, 100), :].astype(F32)

    dq, dret, tgt_t = mix, outgo, tkv
    dkv = (wo_v.at[pl.ds(0, 512)], wo_v.at[pl.ds(512, 512)], dkv_last)

    def attend_back(j):
        base = pl.multiple_of(j * 256, 256)
        datt[...] = dot(wot_v[pl.ds(base, 256), :], dmix[...])

        def head(at):
            hh = lax.div(at, 1024 // LANES)
            lanes = pl.ds(pl.multiple_of(lax.rem(at, 1024 // LANES) * LANES, LANES), LANES)
            local = pl.ds(pl.multiple_of(hh * 64, 64), 64)
            vlocal = pl.ds(pl.multiple_of(256 + hh * 64, 64), 64)
            rows = pl.ds(pl.multiple_of(base + hh * 64, 64), 64)
            vrows = pl.ds(pl.multiple_of(1024 + base + hh * 64, 64), 64)
            grad = datt[local, lanes]
            query = qt[rows, lanes].astype(F32)
            weight = [wts[4 * j + hh, e:e + 1, lanes] for e in range(3)]
            d_weight = [
                jnp.sum(grad * kvg[e, vrows, lanes].astype(F32), axis=0, keepdims=True)
                for e in range(3)
            ]
            inner = weight[0] * d_weight[0] + weight[1] * d_weight[1] + weight[2] * d_weight[2]
            out = None
            for e in range(3):
                d_score = weight[e] * (d_weight[e] - inner) * 0.125
                term = d_score * kvg[e, rows, lanes].astype(F32)
                out = term if out is None else out + term
                dkv[e][local, lanes] = (d_score * query).astype(BF16)
                dkv[e][vlocal, lanes] = (weight[e].astype(BF16).astype(F32) * grad).astype(BF16)
            dq[rows, lanes] = out.astype(BF16)
        blocks(4 * (1024 // LANES), head)

    def gradients(n, j):
        base = pl.multiple_of(j * 256, 256)
        spans = (pl.ds(base, 256), pl.ds(pl.multiple_of(1024 + base, 256), 256))
        for which, span in enumerate(spans):
            rows = pl.ds(256 * which, 256)
            total = dot(dkv[0][rows, :], oht[0])
            for e in range(1, 3):
                total = total + dot(dkv[e][rows, :], oht[e])
            tgt_t[span, :] = total.astype(BF16)
        for target_ref, cols in ((sets[n][0], other_cols), (sets[n][2], own_cols)):
            store_unit(target_ref, 0, dot(dq[spans[0], :], grid_v[:, cols]), True)
            for which, span in enumerate(spans):
                store_unit(target_ref, 1 + which, dot(tgt_t[span, :], th[:, cols]), False)
            if target_ref is sets[n][0]:
                core_copy(n).start()

    background = {
        1: (start_f2, lambda: start_two(0)),
        2: (start_f3, lambda: start_one(1), lambda: start_x(0)),
        3: (start_f4, lambda: start_two(1), lambda: start_one(2)),
        4: (lambda: start_x(1), lambda: start_two(2), lambda: start_one(3)),
    }
    for n in range(1, 5):
        j = lax.rem(x + n, 4)
        attend_back(j)
        for task in background[n]:
            task()
        gradients(n, j)

    table = tgt_t[...].T
    dret[...] = dot(table[128:], wkv_v[...]).astype(BF16)

    def back_copy(r):
        return remote(
            dret.at[pl.ds(32 * r, 32)], drecv.at[pl.ds(32 * (3 - r), 32)],
            back_s.at[r], back_r.at[3 - r], halo_peer(OFFSETS[r]),
        )

    for r in range(4):
        back_copy(r).start()
    start_one(4)
    start_x(2)
    start_two(3)
    own_hidden = dot(table[:128], wkv_v[...])

    stage = att

    def out_copy(at):
        span = pl.ds(pl.multiple_of(at * 256, 256), 256)
        return pltpu.make_async_copy(stage.at[span], dgrid_hbm.at[span], out_sem.at[at])

    def grid_grad(at):
        span = pl.ds(pl.multiple_of(at * 256, 256), 256)
        through = dot(dq[:, span].T, wq_v[...])
        direct = dot(dpf[:, span].T, wfp[...]).astype(BF16).astype(F32)
        stage[span, :] = (direct + through).astype(BF16)
        out_copy(at).start()

    grid_grad(0)
    start_two(4)
    start_x(3)
    blocks(3, lambda at: grid_grad(at + 1))
    for r in range(4):
        back_copy(r).wait()
    dhid_ref[...] = (own_hidden + dot(halo_hot.T, drecv[...])).astype(BF16)
    start_x(4)
    end_f4()
    for n in range(5):
        end_x(n)
    for kind in range(3):
        for by in range(1, 8):
            source = member_peer(by)
            remote(rx.at[kind, source], rx.at[kind, source], x_s.at[0, 0],
                   x_r.at[kind, source], (source, mp)).wait_recv()

    def member_sum(kind, half):
        total = rx[kind, half].astype(F32)
        for other_x in range(1, 4):
            total = total + rx[kind, 2 * other_x + half].astype(F32)
        return total * norm

    for half in range(2):
        cols = slice(512 * half, 512 * half + 512)
        for kind, ref in ((0, go_ref), (1, gq_ref)):
            total = member_sum(kind, half)
            ref[:, cols] = jnp.where(c == 0, total[:8], total[8:])
        gkv_ref[:, cols] = member_sum(2, half)
    for at in range(4):
        out_copy(at).wait()


def on_device(
    hidden, grid_emb, targets, area_w, field_w, edge_table, halo_rows,
    w_query, w_keyval, w_attn_out, w_fields,
):
    def vm(*shape, dtype=BF16):
        return pltpu.VMEM(shape, dtype)

    def sems(*shape):
        return pltpu.SemaphoreType.DMA(shape)

    def comm(lead, count):
        return [
            vm(*lead, 2, count, 256, 256), vm(*lead, 2, 3, count, 64, 256),
            vm(*lead, 2, count, 64, 256), vm(*lead, 2, 3, count, 16, 256),
            vm(*lead, count, 16, 512),
        ]

    square = (1024, 1024)
    scratch = [
        vm(*square), vm(*square), vm(2048, 1024), vm(*square), vm(*square),
        vm(*square), vm(*square), vm(*square), vm(*square),
        vm(256, 1024), vm(2048, 256), vm(3, 1024, 256), vm(3, 2048, 1024),
        vm(16, 8, 1024, dtype=F32),
        vm(128, 1024), vm(1024, 128), vm(FIELD_ROWS, 128, dtype=F32),
        vm(8, FIELD_ROWS, 128, dtype=F32), vm(8, FIELD_ROWS, 128, dtype=F32),
        vm(8, FIELD_ROWS, 128), vm(8, FIELD_ROWS, 128), vm(128, 1024),
        vm(256, 1024, dtype=F32), vm(512, 1024),
        vm(128, 1024), vm(128, 1024),
        vm(8, FIELD_ROWS, 128), vm(8, FIELD_ROWS, 128), vm(4, FIELD_ROWS, 128),
        vm(4, FIELD_ROWS, 128), vm(8, FIELD_ROWS, 128),
        vm(2, 4, 256, 256), vm(2, 2, 4, 256, 256), *comm((), 4), *comm((4,), 3),
        vm(3, 8, 16, 512),
        sems(5), sems(4), sems(4), sems(8), sems(8), sems(8), sems(8), sems(4), sems(4),
        sems(8), sems(8), sems(4), sems(4), sems(4), sems(4), sems(8), sems(8),
        sems(5), sems(5), sems(5, 2, 3), sems(5, 2, 3), sems(5, 2, 3), sems(5, 2, 3),
        sems(5, 8), sems(3, 8), sems(4),
    ]
    vmem = pl.BlockSpec(memory_space=pltpu.VMEM)
    hbm = pl.BlockSpec(memory_space=pl.ANY)
    outs = pl.pallas_call(
        kernel,
        out_shape=(
            jax.ShapeDtypeStruct((128, 1024), BF16),
            jax.ShapeDtypeStruct(square, BF16),
            jax.ShapeDtypeStruct((8, 1024), F32),
            jax.ShapeDtypeStruct((16, 1024), F32),
            jax.ShapeDtypeStruct((8, 1024), F32),
            jax.ShapeDtypeStruct((100, 1024), F32),
        ),
        in_specs=[hbm, hbm, vmem, vmem, vmem, vmem, vmem, hbm, hbm, hbm, vmem],
        out_specs=(vmem, hbm, vmem, vmem, vmem, vmem),
        scratch_shapes=scratch,
        compiler_params=pltpu.CompilerParams(
            collective_id=0, has_side_effects=True, vmem_limit_bytes=63 * 1024 * 1024
        ),
        cost_estimate=pl.CostEstimate(
            flops=22_000_000_000, bytes_accessed=16_000_000, transcendentals=500_000
        ),
        name="decoder_backward",
    )(
        hidden[0], grid_emb[0], targets, area_w.reshape(1, 1024),
        jnp.pad(field_w, (0, FIELD_ROWS - 100)).reshape(FIELD_ROWS, 1),
        edge_table, halo_rows.reshape(128, 1),
        w_query, w_keyval, w_attn_out, w_fields,
    )
    return (outs[0][None], outs[1][None], *outs[2:])


def solution(mesh):
    in_specs = (
        P("member", "mp", None),
        P("member", "mp", None),
        P(None, "mp"),
        P("mp"),
        P(),
        P("mp", None),
        P("mp", None),
        P(),
        P(),
        P(),
        P(),
    )
    out_specs = (
        P("member", "mp", None),
        P("member", "mp", None),
        P(("member", "mp"), None),
        P(("member", "mp"), None),
        P(("member", "mp"), None),
        P(),
    )
    return jax.shard_map(
        on_device, mesh=mesh, in_specs=in_specs, out_specs=out_specs, check_vma=False
    )
```

```python
import math

import jax
import jax.numpy as jnp
from jax import lax
from jax.experimental import pallas as pl
from jax.experimental.pallas import tpu as pltpu
from jax.sharding import PartitionSpec as P

ALPHA_FAIR = 0.95
KAPPA = 0.1
OFFSETS = (-2, -1, 1, 2)
MEMBERS = 8
FIELD_ROWS = 112
TILE = 512
MESH = pl.DeviceIdType.MESH
BF16 = jnp.bfloat16
F32 = jnp.float32
NT = (((1,), (1,)), ((), ()))
NN = (((1,), (0,)), ((), ()))


def dot(left, right, numbers=NN):
    return lax.dot_general(left, right, numbers, preferred_element_type=F32)


def soft_sign(value):
    return value * lax.rsqrt(value * value + KAPPA * KAPPA)


def blocks(count, body, unroll=1):
    def step(at, carry):
        body(at)
        return carry

    lax.fori_loop(0, count, step, 0, unroll=unroll)


def part(at, size, base=0):
    return pl.ds(pl.multiple_of(base + at * size, size), size)


def kernel(
    hid_hbm, grid_hbm, tgt_ref, area_ref, field_ref, edge_ref, halo_ref,
    wq_hbm, wkv_hbm, wo_hbm, wf_ref,
    dhid_ref, dgrid_hbm, gq_ref, gkv_ref, go_ref, gf_ref,
    grid_v, wq_v, wkv_v, wo_v, wot_v, tgrid, qt, att, mix, th, tkv, oh, kvg, wts,
    wfp, wft, frow, fcol, tpad, preds, predr, dps, dpf,
    datt, dkv_last, outgo, hall, dq,
    drecv, dkfull, kvr, kvh, direct,
    fs, fr1, fr2, fr3, fr4,
    w_g, w_recv, w_r1, w_s1, w_r2, w_fin,
    h_g, h_recv, h_r1, h_s1, h_r2, h_fin,
    k_own, k_r1, k_s1, k_r2,
    rx,
    load_sem, halo_s, halo_r, all_s, all_r, ps_s, ps_r, dp_s, dp_r, back_s, back_r, kv_s, kv_r,
    kvh_s, kvh_r, direct_s, direct_r,
    f1_s, f1_r, f2_s, f2_r, f3_s, f3_r, f4_s, f4_r,
    core_s, core_r, one_s, one_r, two_s, two_r, x_s, x_r, out_sem,
):
    me = lax.axis_index("member")
    mp = lax.axis_index("mp")
    x, c = lax.div(me, 2), lax.rem(me, 2)
    y, z = lax.div(mp, 4), lax.rem(mp, 4)
    other = 1 - c
    sibling = (2 * x + other, mp)
    norm = 1.0 / math.sqrt(MEMBERS * 16384.0)

    def halo_peer(by):
        return (me, lax.rem(mp + by + 16, 16))

    def member_peer(by):
        return lax.rem(me + by, 8)

    def x_peer(by):
        return 2 * lax.rem(x + by, 4) + c

    def y_peer(by):
        return (me, 4 * lax.rem(y + by, 4) + z)

    def z_peer(by):
        return (me, 4 * y + lax.rem(z + by, 4))

    def remote(src, dst, send, recv, device):
        return pltpu.make_async_remote_copy(
            src_ref=src, dst_ref=dst, send_sem=send, recv_sem=recv,
            device_id=device, device_id_type=MESH,
        )

    loads = [
        pltpu.make_async_copy(src, dst, load_sem.at[n])
        for n, (src, dst) in enumerate((
            (hid_hbm, th.at[pl.ds(0, 128)]), (grid_hbm, grid_v), (wq_hbm, wq_v),
            (wkv_hbm, wkv_v), (wo_hbm, wo_v), (hid_hbm, hall.at[part(me, 128)]),
        ))
    ]
    for load in loads:
        load.start()
    barrier = pltpu.get_barrier_semaphore()
    partners = (
        [(me, lax.rem(mp + by, 16)) for by in range(1, 16)]
        + [(member_peer(by), mp) for by in range(1, 8)]
        + [(member_peer(by), halo_peer(far)[1]) for by in range(1, 8) for far in OFFSETS]
    )
    for partner in partners:
        pl.semaphore_signal(barrier, inc=1, device_id=partner, device_id_type=MESH)

    for e in range(3):
        oh[e] = (
            lax.broadcasted_iota(jnp.int32, (256, 1024), 0) == edge_ref[e:e + 1, :]
        ).astype(BF16)
    wfp[...] = jnp.zeros_like(wfp)
    wfp[pl.ds(0, 100), :] = wf_ref[...]
    wft[...] = wfp[...].T
    tpad[...] = jnp.zeros_like(tpad)
    tpad[pl.ds(0, 100), :] = tgt_ref[...]
    frow[...] = jnp.zeros_like(frow)
    frow[pl.ds(0, 1), pl.ds(0, 100)] = field_ref[...]
    fcol[...] = jnp.broadcast_to(frow[pl.ds(0, 1), :], (128, 128)).T

    halo_row = jnp.concatenate([halo_ref[l:l + 1, :] for l in range(4)], axis=1)
    halo_home = (
        lax.broadcasted_iota(jnp.int32, (128, 128), 0) == halo_row
    ).astype(BF16)
    loads[0].wait()
    outgo[...] = dot(halo_home.T, th[pl.ds(0, 128), :]).astype(BF16)
    pl.semaphore_wait(barrier, len(partners))
    halos = []
    for l, by in enumerate(OFFSETS):
        copy = remote(
            outgo.at[pl.ds(32 * l, 32)], th.at[pl.ds(128 + 32 * (3 - l), 32)],
            halo_s.at[l], halo_r.at[3 - l], halo_peer(by),
        )
        copy.start()
        halos.append(copy)

    def share(source, at, device):
        return remote(
            hall.at[part(source, 128)] if at > 3 else th.at[pl.ds(0, 128)],
            hall.at[part(source, 128)], all_s.at[at], all_r.at[source], device,
        )

    for by in (1, 3, 2):
        share(me, by, (x_peer(by), mp)).start()
    share(me, 0, sibling).start()

    loads[1].wait()

    def turn(at):
        tgrid[:, part(at, 256)] = grid_v[part(at, 256), :].T
    blocks(4, turn)
    loads[2].wait()
    for at in range(2):
        lanes = pl.ds(TILE * at, TILE)
        qt[:, lanes] = dot(wq_v[...], tgrid[:, lanes]).astype(BF16)

    loads[3].wait()
    for copy in halos:
        copy.wait()

    def make_table(at):
        tkv[part(at, 512), :] = dot(wkv_v[part(at, 512), :], th[...], NT).astype(BF16)
    blocks(4, make_table)

    def gather(t):
        lanes = pl.ds(t * TILE, TILE)
        for e in range(3):
            def rows_of(at, e=e):
                kvg[e, part(at, 512), lanes] = dot(
                    tkv[part(at, 512), :], oh[e, :, lanes]
                ).astype(BF16)
            blocks(4, rows_of)

    def attend(t):
        lanes = pl.ds(t * TILE, TILE)

        def head(h):
            rows, vrows = part(h, 64), part(h, 64, 1024)
            query = qt[rows, lanes].astype(F32)
            raised = []
            for e in range(3):
                key = kvg[e, rows, lanes].astype(F32)
                raised.append(jnp.exp(jnp.sum(query * key, axis=0, keepdims=True) * 0.125))
            total = raised[0] + raised[1] + raised[2]
            out = None
            for e in range(3):
                weight = raised[e] / total
                wts[h, e:e + 1, lanes] = weight
                term = weight.astype(BF16).astype(F32) * kvg[e, vrows, lanes].astype(F32)
                out = term if out is None else out + term
            att[rows, lanes] = out.astype(BF16)
        blocks(16, head, 2)

    def pred_copy(t, by):
        target = member_peer(by)
        return remote(
            preds.at[t, part(target, 16)], predr.at[t, me], ps_s.at[t, by], ps_r.at[t, me],
            (target, mp),
        )

    def predict(t):
        lanes = pl.ds(t * TILE, TILE)
        mixed = (tgrid[:, lanes].astype(F32) + dot(wo_v[...], att[:, lanes])).astype(BF16)
        mix[:, lanes] = mixed
        preds[t] = dot(wfp[...], mixed)
        for by in range(1, 8):
            pred_copy(t, by).start()
        predr[t, me] = preds[t, part(me, 16), :]

    fair = (1.0 - (1.0 - ALPHA_FAIR) / MEMBERS) / (MEMBERS * (MEMBERS - 1))
    mine = part(me, 16)

    def dp_copy(t, by):
        target = member_peer(by)
        return remote(
            dps.at[t, target], dpf.at[mine, pl.ds(t * TILE, TILE)],
            dp_s.at[t, by], dp_r.at[t, me], (target, mp),
        )

    def crps(t):
        for by in range(1, 8):
            source = member_peer(by)
            remote(preds.at[t, part(source, 16)], predr.at[t, source], ps_s.at[t, by],
                   ps_r.at[t, source], (source, mp)).wait_recv()
            pred_copy(t, by).wait_send()
        for chunk in range(TILE // 128):
            lanes = pl.ds(128 * chunk, 128)
            points = pl.ds(t * TILE + 128 * chunk, 128)
            truth = tpad[mine, points]
            scale = fcol[mine, :] * area_ref[:, points]
            pred = [predr[t, m, :, lanes] for m in range(MEMBERS)]
            spread = [jnp.zeros((16, 128), F32) for _ in range(MEMBERS)]
            for i in range(MEMBERS):
                for j in range(i + 1, MEMBERS):
                    term = soft_sign(pred[i] - pred[j])
                    spread[i] = spread[i] + term
                    spread[j] = spread[j] - term
            for m in range(MEMBERS):
                dps[t, m, :, lanes] = (
                    scale * (soft_sign(pred[m] - truth) * (1.0 / MEMBERS) - fair * spread[m])
                ).astype(BF16)
        for by in range(1, 8):
            dp_copy(t, by).start()
        dpf[mine, pl.ds(t * TILE, TILE)] = dps[t, me]

    dmix = tgrid

    def make_dmix(t):
        lanes = pl.ds(t * TILE, TILE)
        for by in range(1, 8):
            source = member_peer(by)
            remote(dps.at[t, source], dpf.at[part(source, 16), lanes], dp_s.at[t, by],
                   dp_r.at[t, source], (source, mp)).wait_recv()
            dp_copy(t, by).wait_send()

        def rows_of(at):
            dmix[part(at, 512), lanes] = dot(wft[part(at, 512), :], dpf[:, lanes]).astype(BF16)
        blocks(2, rows_of)

    gather(0)
    loads[4].wait()
    attend(0)
    predict(0)
    gather(1)
    crps(0)
    attend(1)
    predict(1)

    def turn_out(at):
        wot_v[:, part(at, 256)] = wo_v[part(at, 256), :].T
    blocks(4, turn_out)
    for by in range(1, 4):
        source = x_peer(by)
        share(me, by, (x_peer(by), mp)).wait_send()
        share(source, 0, sibling).wait_recv()
        share(source, 3 + by, sibling).start()
    share(me, 0, sibling).wait_send()
    crps(1)

    dkv = (wo_v.at[pl.ds(0, 512)], wo_v.at[pl.ds(512, 512)], dkv_last)

    def block_of(n):
        return lax.rem(x + n, 4)

    def attend_back(n, tiles):
        j = block_of(n)
        base = pl.multiple_of(j * 256, 256)
        span = pl.ds(tiles[0] * TILE, len(tiles) * TILE)
        datt[:, span] = dot(wot_v[pl.ds(base, 256), :], dmix[:, span])
        for t in tiles:
            lanes = pl.ds(t * TILE, TILE)

            def head(hh):
                local, vlocal = part(hh, 64), part(hh, 64, 256)
                rows = pl.ds(pl.multiple_of(base + hh * 64, 64), 64)
                vrows = pl.ds(pl.multiple_of(1024 + base + hh * 64, 64), 64)
                grad = datt[local, lanes]
                query = qt[rows, lanes].astype(F32)
                weight = [wts[4 * j + hh, e:e + 1, lanes] for e in range(3)]
                d_weight = [
                    jnp.sum(grad * kvg[e, vrows, lanes].astype(F32), axis=0, keepdims=True)
                    for e in range(3)
                ]
                inner = (
                    weight[0] * d_weight[0] + weight[1] * d_weight[1] + weight[2] * d_weight[2]
                )
                out = None
                for e in range(3):
                    d_score = weight[e] * (d_weight[e] - inner) * 0.125
                    term = d_score * kvg[e, rows, lanes].astype(F32)
                    out = term if out is None else out + term
                    dkv[e][local, lanes] = (d_score * query).astype(BF16)
                    dkv[e][vlocal, lanes] = (
                        weight[e].astype(BF16).astype(F32) * grad
                    ).astype(BF16)
                dq[rows, lanes] = out.astype(BF16)
            blocks(4, head)

    def kv_targets(n):
        j = block_of(n)
        return (j, 4 + j)

    def kv_copy(n, which):
        target = kv_targets(n)[which]
        return remote(
            dkfull.at[pl.ds(0, 128), part(target, 256)], kvr.at[part(me, 128)],
            kv_s.at[n - 1, which], kv_r.at[me], (target, mp),
        )

    def kvh_copy(n, which, r):
        target = kv_targets(n)[which]
        return remote(
            dkfull.at[pl.ds(128 + 32 * r, 32), part(target, 256)],
            kvh.at[pl.ds(pl.multiple_of(me * 128 + 32 * (3 - r), 32), 32)],
            kvh_s.at[n - 1, which, r], kvh_r.at[me, 3 - r],
            (target, halo_peer(OFFSETS[r])[1]),
        )

    def scatter(n):
        total = dot(oh[0], dkv[0][...], NT)
        for e in range(1, 3):
            total = total + dot(oh[e], dkv[e][...], NT)
        for which in range(2):
            target = kv_targets(n)[which]
            piece = total[:, 256 * which:256 * which + 256].astype(BF16)
            dkfull[:, part(target, 256)] = piece

            @pl.when(target != me)
            def _():
                kv_copy(n, which).start()

            @pl.when(target == me)
            def _():
                kvr[part(me, 128), :] = piece[:128]

            for r in range(4):
                kvh_copy(n, which, r).start()

    def wait_keyval():
        for by in range(1, 8):
            source = member_peer(by)
            remote(kvr.at[part(source, 128)], kvr.at[part(source, 128)], kv_s.at[0, 0],
                   kv_r.at[source], (source, mp)).wait_recv()
        for source in range(MEMBERS):
            for r in range(4):
                rows = pl.ds(source * 128 + 32 * r, 32)
                remote(kvh.at[rows], kvh.at[rows], kvh_s.at[0, 0, r], kvh_r.at[source, r],
                       halo_peer(OFFSETS[r])).wait_recv()

    def end_keyval():
        for n in range(1, 5):
            for which in range(2):
                @pl.when(kv_targets(n)[which] != me)
                def _():
                    kv_copy(n, which).wait_send()

                for r in range(4):
                    kvh_copy(n, which, r).wait_send()

    def ring(half, by):
        return y_peer(by) if half == 0 else z_peer(by)

    def store_unit(ref, unit, value, crossed=True):
        for core in range(2):
            for half in range(2):
                at = 512 * core + 256 * half
                piece = value[:, at:at + 256].reshape(2, 4, 4, 8, 256)
                order = (2, 1, 0, 3, 4) if half == 1 and crossed else (1, 2, 0, 3, 4)
                ref[core, half, unit] = piece.transpose(order).reshape(256, 256).astype(BF16)

    units = [4, 1, 1, 1, 1, 1]
    sets = [(w_g, w_recv, w_g.at[c], w_r1, w_s1, w_r2, w_fin)] + [
        (h_g.at[n], h_recv.at[n], h_g.at[n, c], h_r1.at[n], h_s1.at[n], h_r2.at[n], h_fin.at[n])
        for n in range(4)
    ] + [(None, None, k_own, k_r1, k_s1, k_r2, None)]

    def core_copy(n):
        return remote(sets[n][0].at[other], sets[n][1], core_s.at[n], core_r.at[n], sibling)

    def one_copy(n, half, by):
        first = lax.rem((y if half == 0 else z) + by, 4)
        return remote(
            sets[n][2].at[half, :, part(first, 64), :], sets[n][3].at[half, by - 1],
            one_s.at[n, half, by - 1], one_r.at[n, half, by - 1], ring(half, by),
        )

    def two_copy(n, half, by):
        second = lax.rem((z if half == 0 else y) + by, 4)
        return remote(
            sets[n][4].at[half, :, part(second, 16), :], sets[n][5].at[half, by - 1],
            two_s.at[n, half, by - 1], two_r.at[n, half, by - 1], ring(1 - half, by),
        )

    def add_cores(n, half):
        own, recv = sets[n][2], sets[n][1]

        def add(unit):
            own[half, unit] = (
                own[half, unit].astype(F32) + recv[half, unit].astype(F32)
            ).astype(BF16)
        blocks(units[n], add)

    def start_one(n):
        core_copy(n).wait()
        for half in range(2):
            add_cores(n, half)
            for by in (2, 1, 3):
                one_copy(n, half, by).start()

    def direct_copy(by):
        target = lax.rem(mp + by, 16)
        return remote(
            sets[4][2].at[:, 0, part(target, 16), :], direct.at[by - 1],
            direct_s.at[by - 1], direct_r.at[by - 1], (me, target),
        )

    def start_direct():
        core_copy(4).wait()
        for half in range(2):
            add_cores(4, half)
        for by in (10, 6, 9, 7, 8, 5, 11, 2, 14, 3, 13, 1, 15, 4, 12):
            direct_copy(by).start()

    def end_direct():
        for by in range(1, 16):
            direct_copy(by).wait()
        for half in range(2):
            total = sets[4][2][half, 0, part(mp, 16), :].astype(F32)
            for by in range(1, 16):
                total = total + direct[by - 1, half].astype(F32)
            sets[4][6][0, :, 256 * half:256 * half + 256] = total.astype(BF16)
        send_x(4)

    def start_two(n):
        own, r1, s1 = sets[n][2], sets[n][3], sets[n][4]
        for half in range(2):
            for by in (1, 3, 2):
                one_copy(n, half, by).wait()
            first = part(y if half == 0 else z, 64)
            for unit in range(units[n]):
                total = own[half, unit, first, :].astype(F32)
                for slot in range(3):
                    total = total + r1[half, slot, unit].astype(F32)
                s1[half, unit] = total.astype(BF16)
            for by in (2, 1, 3):
                two_copy(n, half, by).start()

    def finish_two(n, half, unit):
        total = sets[n][4][half, unit, part(z if half == 0 else y, 16), :].astype(F32)
        for slot in range(3):
            total = total + sets[n][5][half, slot, unit].astype(F32)
        return total

    def x_targets(n):
        if n == 0:
            return [(0, i, 2 * i + k) for i in range(4) for k in range(2)]
        j = block_of(n)
        return [(1, 0, 2 * j), (1, 0, 2 * j + 1)]

    def x_copy(n, index, kind, unit, target):
        return remote(
            sets[n][6].at[unit], rx.at[kind, me], x_s.at[n, index], x_r.at[kind, me],
            (target, mp),
        )

    def start_x(n):
        fin = sets[n][6]
        for half in range(2):
            for by in (1, 3, 2):
                two_copy(n, half, by).wait()
            for unit in range(units[n]):
                fin[unit, :, 256 * half:256 * half + 256] = finish_two(n, half, unit).astype(BF16)
        send_x(n)

    def send_x(n):
        fin = sets[n][6]
        for index, (kind, unit, target) in enumerate(x_targets(n)):
            @pl.when(target != me)
            def _():
                x_copy(n, index, kind, unit, target).start()

            @pl.when(target == me)
            def _():
                rx[kind, me] = fin[unit]

    def end_x(n):
        for index, (kind, unit, target) in enumerate(x_targets(n)):
            @pl.when(target != me)
            def _():
                x_copy(n, index, kind, unit, target).wait_send()

    def query_grad(n):
        span = part(block_of(n), 256)
        store_unit(sets[n][0], 0, dot(dq[span, :], grid_v[...]), n < 4)
        core_copy(n).start()

    def f1_copy(by):
        target = member_peer(by)
        return remote(fs.at[target], fr1.at[me], f1_s.at[by], f1_r.at[me], (target, mp))

    def f2_copy(by):
        return remote(fr2.at[y], fr2.at[y], f2_s.at[by], f2_r.at[y], y_peer(by))

    def f3_copy(by):
        return remote(fr3.at[z], fr3.at[z], f3_s.at[by], f3_r.at[z], z_peer(by))

    def f4_copy(by):
        return remote(fr4.at[me], fr4.at[me], f4_s.at[by], f4_r.at[me], (member_peer(by), mp))

    def slots_sum(ref, count):
        total = ref[0].astype(F32)
        for slot in range(1, count):
            total = total + ref[slot].astype(F32)
        return total

    def start_f2():
        for by in range(1, 8):
            source = member_peer(by)
            remote(fs.at[source], fr1.at[source], f1_s.at[by], f1_r.at[source],
                   (source, mp)).wait_recv()
            f1_copy(by).wait_send()
        fr2[y] = slots_sum(fr1, 8).astype(BF16)
        for by in range(1, 4):
            f2_copy(by).start()

    def start_f3():
        for by in range(1, 4):
            source = lax.rem(y + by, 4)
            remote(fr2.at[source], fr2.at[source], f2_s.at[by], f2_r.at[source],
                   y_peer(by)).wait_recv()
            f2_copy(by).wait_send()
        fr3[z] = slots_sum(fr2, 4).astype(BF16)
        for by in range(1, 4):
            f3_copy(by).start()

    def start_f4():
        for by in range(1, 4):
            source = lax.rem(z + by, 4)
            remote(fr3.at[source], fr3.at[source], f3_s.at[by], f3_r.at[source],
                   z_peer(by)).wait_recv()
            f3_copy(by).wait_send()
        fr4[me] = (slots_sum(fr3, 4) * norm).astype(BF16)
        for by in range(1, 8):
            f4_copy(by).start()

    def end_f4():
        for by in range(1, 8):
            source = member_peer(by)
            remote(fr4.at[source], fr4.at[source], f4_s.at[by], f4_r.at[source],
                   (source, mp)).wait_recv()
            f4_copy(by).wait_send()
        for j in range(MEMBERS):
            gf_ref[:, 128 * j:128 * j + 128] = fr4[j, pl.ds(0, 100), :].astype(F32)

    make_dmix(0)
    attend_back(1, (0,))
    make_dmix(1)

    for at in range(2):
        value = dot(dmix[pl.ds(512 * at, 512), :], att[...], NT)
        for k in range(2):
            store_unit(w_g, 2 * at + k, value[256 * k:256 * k + 256])
    core_copy(0).start()
    g_fields = dot(dpf[pl.ds(0, FIELD_ROWS), :], mix[...], NT)
    for j in range(MEMBERS):
        fs[j] = g_fields[:, 128 * j:128 * j + 128].astype(BF16)
    for by in range(1, 8):
        f1_copy(by).start()
    fr1[me] = fs[me]

    attend_back(1, (1,))
    scatter(1)
    start_one(0)
    attend_back(2, (0, 1))
    scatter(2)
    query_grad(1)
    attend_back(3, (0, 1))
    start_f2()
    start_one(1)
    scatter(3)
    query_grad(2)
    start_two(0)
    attend_back(4, (0, 1))
    start_f3()
    start_one(2)
    scatter(4)
    query_grad(3)
    query_grad(4)
    start_two(1)
    start_x(0)

    def back_copy(r):
        return remote(
            outgo.at[pl.ds(32 * r, 32)], drecv.at[pl.ds(32 * (3 - r), 32)],
            back_s.at[r], back_r.at[3 - r], halo_peer(OFFSETS[r]),
        )

    through_kv = dot(dkfull[...], wkv_v[...])
    outgo[...] = through_kv[128:].astype(BF16)
    own_hidden = through_kv[:128]
    for r in range(4):
        back_copy(r).start()
    start_one(3)
    start_direct()

    stage = att

    def out_copy(at):
        return pltpu.make_async_copy(
            stage.at[part(at, 256)], dgrid_hbm.at[part(at, 256)], out_sem.at[at]
        )

    def grid_grad(at):
        span = pl.ds(256 * at, 256)
        through = dot(dq[:, span].T, wq_v[...])
        direct = dot(dpf[:, span].T, wfp[...]).astype(BF16).astype(F32)
        stage[span, :] = (direct + through).astype(BF16)
        out_copy(at).start()

    grid_grad(0)
    start_two(2)
    start_f4()
    start_x(1)

    loads[5].wait()
    for by in range(4):
        source = 2 * lax.rem(x + by, 4) + other
        share(source, 0, sibling).wait_recv()
    wait_keyval()
    for m in range(MEMBERS):
        rows = pl.ds(128 * m, 128)
        kvr[rows, :] = (
            kvr[rows, :].astype(F32) + dot(halo_home, kvh[rows, :])
        ).astype(BF16)
    value = dot(kvr[...].T, hall[...])
    k_own[0, 0] = value[:, :512].astype(BF16)
    k_own[1, 0] = (
        value[:, 512:].reshape(4, 4, 16, 512).transpose(1, 0, 2, 3).reshape(256, 512)
    ).astype(BF16)
    for half in range(2):
        for by in (2, 1, 3):
            one_copy(5, half, by).start()

    grid_grad(1)
    start_x(2)
    start_two(3)
    grid_grad(2)
    for r in range(4):
        back_copy(r).wait()
    dhid_ref[...] = (own_hidden + dot(halo_home, drecv[...])).astype(BF16)
    start_two(5)
    grid_grad(3)
    end_direct()
    start_x(3)
    end_f4()
    end_keyval()
    for half in range(2):
        for by in (1, 3, 2):
            two_copy(5, half, by).wait()
        gkv_ref[:, 512 * half:512 * half + 512] = finish_two(5, half, 0) * norm
    for n in range(5):
        end_x(n)
    for by in range(1, 4):
        share(x_peer(by), 3 + by, sibling).wait_send()
    for kind in range(2):
        for by in range(1, 8):
            source = member_peer(by)
            remote(rx.at[kind, source], rx.at[kind, source], x_s.at[0, 0],
                   x_r.at[kind, source], (source, mp)).wait_recv()
    for kind, ref in ((0, go_ref), (1, gq_ref)):
        for half in range(2):
            total = rx[kind, half].astype(F32)
            for by in range(1, 4):
                total = total + rx[kind, 2 * by + half].astype(F32)
            total = total * norm
            ref[:, 512 * half:512 * half + 512] = jnp.where(c == 0, total[:8], total[8:])
    for at in range(4):
        out_copy(at).wait()


def hand_over(*refs):
    count = 6
    sources, targets, held = refs[:count], refs[count:2 * count], refs[2 * count:3 * count]
    in_sems, out_sems = refs[3 * count:]
    pieces = [(1, part(at, 256)) for at in range(4)] + [
        (n, slice(None)) for n in (5, 0, 3, 2, 4)
    ]
    reads = [
        pltpu.make_async_copy(sources[n].at[rows], held[n].at[rows], in_sems.at[i])
        for i, (n, rows) in enumerate(pieces)
    ]
    writes = [
        pltpu.make_async_copy(held[n].at[rows], targets[n].at[rows], out_sems.at[i])
        for i, (n, rows) in enumerate(pieces)
    ]
    for read in reads:
        read.start()
    for read, write in zip(reads, writes):
        read.wait()
        write.start()
    for write in writes:
        write.wait()


def on_device(
    hidden, grid_emb, targets, area_w, field_w, edge_table, halo_rows,
    w_query, w_keyval, w_attn_out, w_fields,
):
    def vm(*shape, dtype=BF16):
        return pltpu.VMEM(shape, dtype)

    def sems(*shape):
        return pltpu.SemaphoreType.DMA(shape)

    def comm(lead, count):
        return [
            vm(*lead, 2, 2, count, 256, 256), vm(*lead, 2, count, 256, 256),
            vm(*lead, 2, 3, count, 64, 256), vm(*lead, 2, count, 64, 256),
            vm(*lead, 2, 3, count, 16, 256), vm(*lead, count, 16, 512),
        ]

    square = (1024, 1024)
    scratch = [
        vm(*square), vm(*square), vm(2048, 1024), vm(*square), vm(*square),
        vm(*square), vm(*square), vm(*square), vm(*square),
        vm(256, 1024), vm(2048, 256), vm(3, 256, 1024), vm(3, 2048, 1024),
        vm(16, 8, 1024, dtype=F32),
        vm(128, 1024), vm(1024, 128), vm(8, 128, dtype=F32), vm(128, 128, dtype=F32),
        vm(128, 1024, dtype=F32), vm(2, 128, TILE, dtype=F32), vm(2, 8, 16, TILE, dtype=F32),
        vm(2, 8, 16, TILE), vm(128, 1024),
        vm(256, 1024, dtype=F32), vm(512, 1024), vm(128, 1024), vm(*square), vm(*square),
        vm(128, 1024), vm(256, 2048), vm(1024, 256), vm(1024, 256), vm(15, 2, 16, 256),
        vm(8, FIELD_ROWS, 128), vm(8, FIELD_ROWS, 128), vm(4, FIELD_ROWS, 128),
        vm(4, FIELD_ROWS, 128), vm(8, FIELD_ROWS, 128),
        *comm((), 4), *comm((4,), 1),
        vm(2, 1, 256, 512), vm(2, 3, 1, 64, 512), vm(2, 1, 64, 512), vm(2, 3, 1, 16, 512),
        vm(2, 8, 16, 512),
        sems(6), sems(4), sems(4), sems(7), sems(8), sems(2, 8), sems(2, 8), sems(2, 8),
        sems(2, 8), sems(4), sems(4), sems(4, 2), sems(8), sems(4, 2, 4), sems(8, 4),
        sems(15), sems(15),
        sems(8), sems(8), sems(4), sems(4), sems(4), sems(4), sems(8), sems(8),
        sems(5), sems(5), sems(6, 2, 3), sems(6, 2, 3), sems(6, 2, 3), sems(6, 2, 3),
        sems(5, 8), sems(2, 8), sems(4),
    ]
    vmem = pl.BlockSpec(memory_space=pltpu.VMEM)
    hbm = pl.BlockSpec(memory_space=pl.ANY)
    shapes = (
        jax.ShapeDtypeStruct((128, 1024), BF16),
        jax.ShapeDtypeStruct(square, BF16),
        jax.ShapeDtypeStruct((8, 1024), F32),
        jax.ShapeDtypeStruct((16, 1024), F32),
        jax.ShapeDtypeStruct((8, 1024), F32),
        jax.ShapeDtypeStruct((100, 1024), F32),
    )
    raw = pl.pallas_call(
        kernel,
        out_shape=shapes,
        in_specs=[hbm, hbm, vmem, vmem, vmem, vmem, vmem, hbm, hbm, hbm, vmem],
        out_specs=(vmem, hbm, vmem, vmem, vmem, vmem),
        scratch_shapes=scratch,
        compiler_params=pltpu.CompilerParams(
            collective_id=0, has_side_effects=True, vmem_limit_bytes=63 * 1024 * 1024
        ),
        cost_estimate=pl.CostEstimate(
            flops=22_000_000_000, bytes_accessed=16_000_000, transcendentals=500_000
        ),
        name="decoder_backward",
    )(
        hidden[0], grid_emb[0], targets, area_w.reshape(1, 1024), field_w.reshape(1, 100),
        edge_table.T, halo_rows, w_query, w_keyval, w_attn_out, w_fields,
    )
    outs = pl.pallas_call(
        hand_over,
        out_shape=shapes,
        in_specs=[hbm] * 6,
        out_specs=(hbm,) * 6,
        scratch_shapes=[pltpu.VMEM(shape.shape, shape.dtype) for shape in shapes]
        + [sems(9), sems(9)],
        compiler_params=pltpu.CompilerParams(vmem_limit_bytes=63 * 1024 * 1024),
        cost_estimate=pl.CostEstimate(flops=0, bytes_accessed=6_000_000, transcendentals=0),
        name="hand_over",
    )(*raw)
    return (outs[0][None], outs[1][None], *outs[2:])


def solution(mesh):
    in_specs = (
        P("member", "mp", None),
        P("member", "mp", None),
        P(None, "mp"),
        P("mp"),
        P(),
        P("mp", None),
        P("mp", None),
        P(),
        P(),
        P(),
        P(),
    )
    out_specs = (
        P("member", "mp", None),
        P("member", "mp", None),
        P(("member", "mp"), None),
        P(("member", "mp"), None),
        P(("member", "mp"), None),
        P(),
    )
    return jax.shard_map(
        on_device, mesh=mesh, in_specs=in_specs, out_specs=out_specs, check_vma=False
    )
```

```python
import math

import jax
import jax.numpy as jnp
from jax import lax
from jax.experimental import pallas as pl
from jax.experimental.pallas import tpu as pltpu
from jax.sharding import PartitionSpec as P

ALPHA_FAIR = 0.95
KAPPA = 0.1
OFFSETS = (-2, -1, 1, 2)
MEMBERS = 8
FIELD_ROWS = 112
TILE = 512
MESH = pl.DeviceIdType.MESH
BF16 = jnp.bfloat16
F32 = jnp.float32
NT = (((1,), (1,)), ((), ()))
NN = (((1,), (0,)), ((), ()))


def dot(left, right, numbers=NN):
    return lax.dot_general(left, right, numbers, preferred_element_type=F32)


def soft_sign(value):
    return value * lax.rsqrt(value * value + KAPPA * KAPPA)


def blocks(count, body, unroll=1):
    def step(at, carry):
        body(at)
        return carry

    lax.fori_loop(0, count, step, 0, unroll=unroll)


def part(at, size, base=0):
    return pl.ds(pl.multiple_of(base + at * size, size), size)


def kernel(
    hid_hbm, grid_hbm, tgt_hbm, area_ref, field_ref, edge_ref, halo_ref,
    wq_hbm, wkv_hbm, wo_hbm, wf_hbm,
    dhid_hbm, dgrid_hbm, gq_ref, gkv_ref, go_ref, gf_hbm,
    tgt_ref, wf_ref, dhid_ref, gf_ref,
    grid_v, wq_v, wkv_v, wo_v, wot_v, tgrid, qt, att, mix, th, tkv, oh, kvg, wts,
    wfp, wft, frow, fcol, tpad, preds, predr, dps, dpf,
    datt, dpart, outgo, hall, dq,
    drecv, dkfull, kvr, kvh, direct,
    fs, fr1, fr2, fr3, fr4,
    w_g, w_recv, w_r1, w_s1, w_r2, w_fin,
    h_g, h_recv, h_r1, h_s1, h_r2, h_fin,
    k_own, k_r1, k_s1, k_r2,
    rx,
    load_sem, halo_s, halo_r, all_s, all_r, ps_s, ps_r, dp_s, dp_r, back_s, back_r, kv_s, kv_r,
    kvh_s, kvh_r, direct_s, direct_r,
    f1_s, f1_r, f2_s, f2_r, f3_s, f3_r, f4_s, f4_r,
    core_s, core_r, one_s, one_r, two_s, two_r, x_s, x_r, out_sem,
):
    me = lax.axis_index("member")
    mp = lax.axis_index("mp")
    x, c = lax.div(me, 2), lax.rem(me, 2)
    y, z = lax.div(mp, 4), lax.rem(mp, 4)
    other = 1 - c
    sibling = (2 * x + other, mp)
    norm = 1.0 / math.sqrt(MEMBERS * 16384.0)

    def halo_peer(by):
        return (me, lax.rem(mp + by + 16, 16))

    def member_peer(by):
        return lax.rem(me + by, 8)

    def x_peer(by):
        return 2 * lax.rem(x + by, 4) + c

    def y_peer(by):
        return (me, 4 * lax.rem(y + by, 4) + z)

    def z_peer(by):
        return (me, 4 * y + lax.rem(z + by, 4))

    def remote(src, dst, send, recv, device):
        return pltpu.make_async_remote_copy(
            src_ref=src, dst_ref=dst, send_sem=send, recv_sem=recv,
            device_id=device, device_id_type=MESH,
        )

    loads = [
        pltpu.make_async_copy(src, dst, load_sem.at[n])
        for n, (src, dst) in enumerate((
            (hid_hbm, th.at[pl.ds(0, 128)]), (grid_hbm, grid_v), (wq_hbm, wq_v),
            (wkv_hbm, wkv_v), (wo_hbm, wo_v), (hid_hbm, hall.at[part(me, 128)]),
            (tgt_hbm, tgt_ref), (wf_hbm, wf_ref),
        ))
    ]
    for load in loads:
        load.start()
    barrier = pltpu.get_barrier_semaphore()
    partners = (
        [halo_peer(by) for by in OFFSETS]
        + [(member_peer(by), mp) for by in range(1, 8)]
        + [y_peer(by) for by in range(1, 4)]
    )
    for partner in partners:
        pl.semaphore_signal(barrier, inc=1, device_id=partner, device_id_type=MESH)

    for e in range(3):
        oh[e] = (
            lax.broadcasted_iota(jnp.int32, (256, 1024), 0) == edge_ref[e:e + 1, :]
        ).astype(BF16)
    loads[7].wait()
    wfp[...] = jnp.zeros_like(wfp)
    wfp[pl.ds(0, 100), :] = wf_ref[...]
    wft[...] = wfp[...].T
    frow[...] = jnp.zeros_like(frow)
    frow[pl.ds(0, 1), pl.ds(0, 100)] = field_ref[...]
    fcol[...] = jnp.broadcast_to(frow[pl.ds(0, 1), :], (128, 128)).T

    halo_row = jnp.concatenate([halo_ref[l:l + 1, :] for l in range(4)], axis=1)
    halo_home = (
        lax.broadcasted_iota(jnp.int32, (128, 128), 0) == halo_row
    ).astype(BF16)
    loads[0].wait()
    outgo[...] = dot(halo_home.T, th[pl.ds(0, 128), :]).astype(BF16)
    pl.semaphore_wait(barrier, len(partners))
    halos = []
    for l, by in enumerate(OFFSETS):
        copy = remote(
            outgo.at[pl.ds(32 * l, 32)], th.at[pl.ds(128 + 32 * (3 - l), 32)],
            halo_s.at[l], halo_r.at[3 - l], halo_peer(by),
        )
        copy.start()
        halos.append(copy)

    def share(source, at, device):
        return remote(
            hall.at[part(source, 128)] if at > 3 else th.at[pl.ds(0, 128)],
            hall.at[part(source, 128)], all_s.at[at], all_r.at[source], device,
        )

    for by in (1, 3, 2):
        share(me, by, (x_peer(by), mp)).start()
    share(me, 0, sibling).start()

    loads[1].wait()

    def turn(at):
        tgrid[:, part(at, 256)] = grid_v[part(at, 256), :].T
    blocks(4, turn)
    loads[2].wait()
    for at in range(2):
        lanes = pl.ds(TILE * at, TILE)
        qt[:, lanes] = dot(wq_v[...], tgrid[:, lanes]).astype(BF16)

    def make_table(first):
        rows = pl.ds(first, 128)

        def rows_of(at):
            tkv[part(at, 512), rows] = dot(wkv_v[part(at, 512), :], th[rows, :], NT).astype(BF16)
        blocks(4, rows_of)

    loads[3].wait()
    make_table(0)
    loads[4].wait()

    def turn_out(at):
        wot_v[:, part(at, 256)] = wo_v[part(at, 256), :].T
    blocks(4, turn_out)
    for copy in halos:
        copy.wait()
    make_table(128)
    loads[6].wait()
    tpad[...] = jnp.zeros_like(tpad)
    tpad[pl.ds(0, 100), :] = tgt_ref[...]

    def gather(t):
        lanes = pl.ds(t * TILE, TILE)
        for e in range(3):
            def rows_of(at, e=e):
                kvg[e, part(at, 512), lanes] = dot(
                    tkv[part(at, 512), :], oh[e, :, lanes]
                ).astype(BF16)
            blocks(4, rows_of)

    def attend(t):
        lanes = pl.ds(t * TILE, TILE)

        def head(h):
            rows, vrows = part(h, 64), part(h, 64, 1024)
            query = qt[rows, lanes].astype(F32)
            raised = []
            for e in range(3):
                key = kvg[e, rows, lanes].astype(F32)
                raised.append(jnp.exp(jnp.sum(query * key, axis=0, keepdims=True) * 0.125))
            total = raised[0] + raised[1] + raised[2]
            out = None
            for e in range(3):
                weight = raised[e] / total
                wts[h, e:e + 1, lanes] = weight
                term = weight.astype(BF16).astype(F32) * kvg[e, vrows, lanes].astype(F32)
                out = term if out is None else out + term
            att[rows, lanes] = out.astype(BF16)
        blocks(16, head, 2)

    def pred_copy(t, by):
        target = member_peer(by)
        return remote(
            preds.at[t, part(target, 16)], predr.at[t, me], ps_s.at[t, by], ps_r.at[t, me],
            (target, mp),
        )

    def predict(t):
        lanes = pl.ds(t * TILE, TILE)
        mixed = (tgrid[:, lanes].astype(F32) + dot(wo_v[...], att[:, lanes])).astype(BF16)
        mix[:, lanes] = mixed
        preds[t] = dot(wfp[...], mixed)
        for by in range(1, 8):
            pred_copy(t, by).start()
        predr[t, me] = preds[t, part(me, 16), :]

    fair = (1.0 - (1.0 - ALPHA_FAIR) / MEMBERS) / (MEMBERS * (MEMBERS - 1))
    mine = part(me, 16)

    def dp_copy(t, by):
        target = member_peer(by)
        return remote(
            dps.at[t, target], dpf.at[mine, pl.ds(t * TILE, TILE)],
            dp_s.at[t, by], dp_r.at[t, me], (target, mp),
        )

    def crps(t):
        for by in range(1, 8):
            source = member_peer(by)
            remote(preds.at[t, part(source, 16)], predr.at[t, source], ps_s.at[t, by],
                   ps_r.at[t, source], (source, mp)).wait_recv()
            pred_copy(t, by).wait_send()
        for chunk in range(TILE // 128):
            lanes = pl.ds(128 * chunk, 128)
            points = pl.ds(t * TILE + 128 * chunk, 128)
            truth = tpad[mine, points]
            scale = fcol[mine, :] * area_ref[:, points]
            pred = [predr[t, m, :, lanes] for m in range(MEMBERS)]
            spread = [jnp.zeros((16, 128), F32) for _ in range(MEMBERS)]
            for i in range(MEMBERS):
                for j in range(i + 1, MEMBERS):
                    term = soft_sign(pred[i] - pred[j])
                    spread[i] = spread[i] + term
                    spread[j] = spread[j] - term
            for m in range(MEMBERS):
                dps[t, m, :, lanes] = (
                    scale * (soft_sign(pred[m] - truth) * (1.0 / MEMBERS) - fair * spread[m])
                ).astype(BF16)
        for by in range(1, 8):
            dp_copy(t, by).start()
        dpf[mine, pl.ds(t * TILE, TILE)] = dps[t, me]

    dmix = tgrid

    def make_dmix(t):
        lanes = pl.ds(t * TILE, TILE)
        for by in range(1, 8):
            source = member_peer(by)
            remote(dps.at[t, source], dpf.at[part(source, 16), lanes], dp_s.at[t, by],
                   dp_r.at[t, source], (source, mp)).wait_recv()
            dp_copy(t, by).wait_send()

        def rows_of(at):
            dmix[part(at, 512), lanes] = dot(wft[part(at, 512), :], dpf[:, lanes]).astype(BF16)
        blocks(2, rows_of)

    gather(0)
    attend(0)
    predict(0)
    gather(1)
    attend(1)
    crps(0)
    predict(1)

    for by in range(1, 4):
        source = x_peer(by)
        share(me, by, (x_peer(by), mp)).wait_send()
        share(source, 0, sibling).wait_recv()
        share(source, 3 + by, sibling).start()
    share(me, 0, sibling).wait_send()

    dkv = [
        wo_v.at[pl.ds(512 * (e // 2), 512), pl.ds(512 * (e % 2), 512)] for e in range(3)
    ]

    def block_of(n):
        return lax.rem(x + n, 4)

    def attend_back(n, t):
        j = block_of(n)
        base = pl.multiple_of(j * 256, 256)
        lanes = pl.ds(t * TILE, TILE)
        datt[...] = dot(wot_v[pl.ds(base, 256), :], dmix[:, lanes])

        def head(hh):
            local, vlocal = part(hh, 64), part(hh, 64, 256)
            rows = pl.ds(pl.multiple_of(base + hh * 64, 64), 64)
            vrows = pl.ds(pl.multiple_of(1024 + base + hh * 64, 64), 64)
            grad = datt[local, :]
            query = qt[rows, lanes].astype(F32)
            weight = [wts[4 * j + hh, e:e + 1, lanes] for e in range(3)]
            d_weight = [
                jnp.sum(grad * kvg[e, vrows, lanes].astype(F32), axis=0, keepdims=True)
                for e in range(3)
            ]
            inner = weight[0] * d_weight[0] + weight[1] * d_weight[1] + weight[2] * d_weight[2]
            out = None
            for e in range(3):
                d_score = weight[e] * (d_weight[e] - inner) * 0.125
                term = d_score * kvg[e, rows, lanes].astype(F32)
                out = term if out is None else out + term
                dkv[e][local, :] = (d_score * query).astype(BF16)
                dkv[e][vlocal, :] = (weight[e].astype(BF16).astype(F32) * grad).astype(BF16)
            dq[rows, lanes] = out.astype(BF16)
        blocks(4, head)
        total = dot(oh[0, :, lanes], dkv[0][...], NT)
        for e in range(1, 3):
            total = total + dot(oh[e, :, lanes], dkv[e][...], NT)
        if t == 0:
            dpart[n - 1] = total
        else:
            send_keyval(n, total + dpart[n - 1])

    def kv_targets(n):
        j = block_of(n)
        return (j, 4 + j)

    def kv_copy(n, which):
        target = kv_targets(n)[which]
        return remote(
            dkfull.at[pl.ds(0, 128), part(target, 256)], kvr.at[part(me, 128)],
            kv_s.at[n - 1, which], kv_r.at[me], (target, mp),
        )

    def kvh_copy(n, which, r):
        target = kv_targets(n)[which]
        return remote(
            dkfull.at[pl.ds(128 + 32 * r, 32), part(target, 256)],
            kvh.at[pl.ds(pl.multiple_of(me * 128 + 32 * (3 - r), 32), 32)],
            kvh_s.at[n - 1, which, r], kvh_r.at[me, 3 - r],
            (target, halo_peer(OFFSETS[r])[1]),
        )

    def send_keyval(n, total):
        for which in range(2):
            target = kv_targets(n)[which]
            piece = total[:, 256 * which:256 * which + 256].astype(BF16)
            dkfull[:, part(target, 256)] = piece

            @pl.when(target != me)
            def _():
                kv_copy(n, which).start()

            @pl.when(target == me)
            def _():
                kvr[part(me, 128), :] = piece[:128]

            for r in range(4):
                kvh_copy(n, which, r).start()

    def wait_keyval():
        for by in range(1, 8):
            source = member_peer(by)
            remote(kvr.at[part(source, 128)], kvr.at[part(source, 128)], kv_s.at[0, 0],
                   kv_r.at[source], (source, mp)).wait_recv()
        for source in range(MEMBERS):
            for r in range(4):
                rows = pl.ds(source * 128 + 32 * r, 32)
                remote(kvh.at[rows], kvh.at[rows], kvh_s.at[0, 0, r], kvh_r.at[source, r],
                       halo_peer(OFFSETS[r])).wait_recv()

    def end_keyval():
        for n in range(1, 5):
            for which in range(2):
                @pl.when(kv_targets(n)[which] != me)
                def _():
                    kv_copy(n, which).wait_send()

                for r in range(4):
                    kvh_copy(n, which, r).wait_send()

    def ring(half, by):
        return y_peer(by) if half == 0 else z_peer(by)

    def store_unit(ref, unit, value, crossed=True):
        for core in range(2):
            for half in range(2):
                at = 512 * core + 256 * half
                piece = value[:, at:at + 256].reshape(2, 4, 4, 8, 256)
                order = (2, 1, 0, 3, 4) if half == 1 and crossed else (1, 2, 0, 3, 4)
                piece = piece.transpose(order).reshape(256, 256)
                ref[core, half, unit] = piece.astype(BF16)

    units = [4, 1, 1, 1, 1, 1]
    sets = [(w_g, w_recv, w_g.at[c], w_r1, w_s1, w_r2, w_fin)] + [
        (h_g.at[n], h_recv.at[n], h_g.at[n, c], h_r1.at[n], h_s1.at[n], h_r2.at[n], h_fin.at[n])
        for n in range(4)
    ] + [(None, None, k_own, k_r1, k_s1, k_r2, None)]

    def core_copy(n):
        return remote(sets[n][0].at[other], sets[n][1], core_s.at[n], core_r.at[n], sibling)

    def one_copy(n, half, by):
        first = lax.rem((y if half == 0 else z) + by, 4)
        return remote(
            sets[n][2].at[half, :, part(first, 64), :], sets[n][3].at[half, by - 1],
            one_s.at[n, half, by - 1], one_r.at[n, half, by - 1], ring(half, by),
        )

    def two_copy(n, half, by):
        second = lax.rem((z if half == 0 else y) + by, 4)
        return remote(
            sets[n][4].at[half, :, part(second, 16), :], sets[n][5].at[half, by - 1],
            two_s.at[n, half, by - 1], two_r.at[n, half, by - 1], ring(1 - half, by),
        )

    def add_cores(n, half):
        own, recv = sets[n][2], sets[n][1]

        def add(unit):
            own[half, unit] = (
                own[half, unit].astype(F32) + recv[half, unit].astype(F32)
            ).astype(BF16)
        blocks(units[n], add)

    def start_one(n):
        core_copy(n).wait()
        for half in range(2):
            add_cores(n, half)
            for by in (2, 1, 3):
                one_copy(n, half, by).start()

    def direct_copy(by):
        target = lax.rem(mp + by, 16)
        return remote(
            sets[4][2].at[:, 0, part(target, 16), :], direct.at[by - 1],
            direct_s.at[by - 1], direct_r.at[by - 1], (me, target),
        )

    def start_direct():
        core_copy(4).wait()
        for half in range(2):
            add_cores(4, half)
        for by in (10, 6, 9, 7, 8, 5, 11, 2, 14, 3, 13, 1, 15, 4, 12):
            direct_copy(by).start()

    def end_direct():
        for by in range(1, 16):
            direct_copy(by).wait()
        for half in range(2):
            total = sets[4][2][half, 0, part(mp, 16), :].astype(F32)
            for by in range(1, 16):
                total = total + direct[by - 1, half].astype(F32)
            sets[4][6][0, :, 256 * half:256 * half + 256] = total.astype(BF16)
        send_x(4)

    def start_two(n):
        own, r1, s1 = sets[n][2], sets[n][3], sets[n][4]
        for half in range(2):
            for by in (1, 3, 2):
                one_copy(n, half, by).wait()
            first = part(y if half == 0 else z, 64)
            for unit in range(units[n]):
                total = own[half, unit, first, :].astype(F32)
                for slot in range(3):
                    total = total + r1[half, slot, unit].astype(F32)
                s1[half, unit] = total.astype(BF16)
            for by in (2, 1, 3):
                two_copy(n, half, by).start()

    def finish_two(n, half, unit):
        total = sets[n][4][half, unit, part(z if half == 0 else y, 16), :].astype(F32)
        for slot in range(3):
            total = total + sets[n][5][half, slot, unit].astype(F32)
        return total

    def x_targets(n):
        if n == 0:
            return [(0, i, 2 * i + k) for i in range(4) for k in range(2)]
        j = block_of(n)
        return [(1, 0, 2 * j), (1, 0, 2 * j + 1)]

    def x_copy(n, index, kind, unit, target):
        return remote(
            sets[n][6].at[unit], rx.at[kind, me], x_s.at[n, index], x_r.at[kind, me],
            (target, mp),
        )

    def start_x(n):
        fin = sets[n][6]
        for half in range(2):
            for by in (1, 3, 2):
                two_copy(n, half, by).wait()
            for unit in range(units[n]):
                fin[unit, :, 256 * half:256 * half + 256] = finish_two(n, half, unit).astype(BF16)
        send_x(n)

    def send_x(n):
        fin = sets[n][6]
        for index, (kind, unit, target) in enumerate(x_targets(n)):
            @pl.when(target != me)
            def _():
                x_copy(n, index, kind, unit, target).start()

            @pl.when(target == me)
            def _():
                rx[kind, me] = fin[unit]

    def end_x(n):
        for index, (kind, unit, target) in enumerate(x_targets(n)):
            @pl.when(target != me)
            def _():
                x_copy(n, index, kind, unit, target).wait_send()

    def query_grad(n):
        span = part(block_of(n), 256)
        store_unit(sets[n][0], 0, dot(dq[span, :], grid_v[...]), n < 4)
        core_copy(n).start()

    def out_grad():
        for at in range(2):
            value = dot(dmix[pl.ds(512 * at, 512), :], att[...], NT)
            for k in range(2):
                store_unit(w_g, 2 * at + k, value[256 * k:256 * k + 256])
        core_copy(0).start()

    def fields_grad():
        value = dot(dpf[pl.ds(0, FIELD_ROWS), :], mix[...], NT)
        for j in range(MEMBERS):
            fs[j] = value[:, 128 * j:128 * j + 128].astype(BF16)
        for by in range(1, 8):
            f1_copy(by).start()
        fr1[me] = fs[me]

    def f1_copy(by):
        target = member_peer(by)
        return remote(fs.at[target], fr1.at[me], f1_s.at[by], f1_r.at[me], (target, mp))

    def f2_copy(by):
        return remote(fr2.at[y], fr2.at[y], f2_s.at[by], f2_r.at[y], y_peer(by))

    def f3_copy(by):
        return remote(fr3.at[z], fr3.at[z], f3_s.at[by], f3_r.at[z], z_peer(by))

    def f4_copy(by):
        return remote(fr4.at[me], fr4.at[me], f4_s.at[by], f4_r.at[me], (member_peer(by), mp))

    def slots_sum(ref, count):
        total = ref[0].astype(F32)
        for slot in range(1, count):
            total = total + ref[slot].astype(F32)
        return total

    def start_f2():
        for by in range(1, 8):
            source = member_peer(by)
            remote(fs.at[source], fr1.at[source], f1_s.at[by], f1_r.at[source],
                   (source, mp)).wait_recv()
            f1_copy(by).wait_send()
        fr2[y] = slots_sum(fr1, 8).astype(BF16)
        for by in range(1, 4):
            f2_copy(by).start()

    def start_f3():
        for by in range(1, 4):
            source = lax.rem(y + by, 4)
            remote(fr2.at[source], fr2.at[source], f2_s.at[by], f2_r.at[source],
                   y_peer(by)).wait_recv()
            f2_copy(by).wait_send()
        fr3[z] = slots_sum(fr2, 4).astype(BF16)
        for by in range(1, 4):
            f3_copy(by).start()

    def start_f4():
        for by in range(1, 4):
            source = lax.rem(z + by, 4)
            remote(fr3.at[source], fr3.at[source], f3_s.at[by], f3_r.at[source],
                   z_peer(by)).wait_recv()
            f3_copy(by).wait_send()
        fr4[me] = (slots_sum(fr3, 4) * norm).astype(BF16)
        for by in range(1, 8):
            f4_copy(by).start()

    def end_f4():
        for by in range(1, 8):
            source = member_peer(by)
            remote(fr4.at[source], fr4.at[source], f4_s.at[by], f4_r.at[source],
                   (source, mp)).wait_recv()
            f4_copy(by).wait_send()
        for j in range(MEMBERS):
            gf_ref[:, 128 * j:128 * j + 128] = fr4[j, pl.ds(0, 100), :].astype(F32)

    make_dmix(0)
    attend_back(1, 0)
    crps(1)
    attend_back(2, 0)
    attend_back(3, 0)
    attend_back(4, 0)
    make_dmix(1)
    out_grad()
    fields_grad()
    attend_back(1, 1)
    start_one(0)
    query_grad(1)
    attend_back(2, 1)
    query_grad(2)
    start_one(1)
    attend_back(3, 1)
    query_grad(3)
    start_f2()
    start_one(2)
    attend_back(4, 1)
    query_grad(4)
    start_one(3)

    def back_copy(r):
        return remote(
            outgo.at[pl.ds(32 * r, 32)], drecv.at[pl.ds(32 * (3 - r), 32)],
            back_s.at[r], back_r.at[3 - r], halo_peer(OFFSETS[r]),
        )

    through_kv = dot(dkfull[...], wkv_v[...])
    outgo[...] = through_kv[128:].astype(BF16)
    own_hidden = through_kv[:128]
    for r in range(4):
        back_copy(r).start()
    start_direct()

    stage = att

    def out_copy(at):
        return pltpu.make_async_copy(
            stage.at[part(at, 256)], dgrid_hbm.at[part(at, 256)], out_sem.at[at]
        )

    def grid_grad(at):
        span = pl.ds(256 * at, 256)
        through = dot(dq[:, span].T, wq_v[...])
        direct = dot(dpf[:, span].T, wfp[...]).astype(BF16).astype(F32)
        stage[span, :] = (direct + through).astype(BF16)
        out_copy(at).start()

    grid_grad(0)
    start_two(0)
    start_two(1)
    grid_grad(1)
    start_f3()

    loads[5].wait()
    for by in range(4):
        source = 2 * lax.rem(x + by, 4) + other
        share(source, 0, sibling).wait_recv()
    wait_keyval()
    for m in range(MEMBERS):
        rows = pl.ds(128 * m, 128)
        kvr[rows, :] = (
            kvr[rows, :].astype(F32) + dot(halo_home, kvh[rows, :])
        ).astype(BF16)
    value = dot(kvr[...].T, hall[...])
    k_own[0, 0] = value[:, :512].astype(BF16)
    k_own[1, 0] = (
        value[:, 512:].reshape(4, 4, 16, 512).transpose(1, 0, 2, 3).reshape(256, 512)
    ).astype(BF16)
    for half in range(2):
        for by in (2, 1, 3):
            one_copy(5, half, by).start()

    start_two(2)
    start_two(3)
    grid_grad(2)
    start_x(0)
    start_x(1)
    for r in range(4):
        back_copy(r).wait()
    dhid_ref[...] = (own_hidden + dot(halo_home, drecv[...])).astype(BF16)
    dhid_out = pltpu.make_async_copy(dhid_ref, dhid_hbm, out_sem.at[4])
    dhid_out.start()
    start_f4()
    grid_grad(3)
    start_two(5)
    start_x(2)
    start_x(3)
    end_direct()
    end_f4()
    gf_out = pltpu.make_async_copy(gf_ref, gf_hbm, out_sem.at[5])
    gf_out.start()
    end_keyval()
    for half in range(2):
        for by in (1, 3, 2):
            two_copy(5, half, by).wait()
        gkv_ref[:, 512 * half:512 * half + 512] = finish_two(5, half, 0) * norm
    for n in range(5):
        end_x(n)
    for by in range(1, 4):
        share(x_peer(by), 3 + by, sibling).wait_send()
    for kind in range(2):
        for by in range(1, 8):
            source = member_peer(by)
            remote(rx.at[kind, source], rx.at[kind, source], x_s.at[0, 0],
                   x_r.at[kind, source], (source, mp)).wait_recv()
    for kind, ref in ((0, go_ref), (1, gq_ref)):
        for half in range(2):
            total = rx[kind, half].astype(F32)
            for by in range(1, 4):
                total = total + rx[kind, 2 * by + half].astype(F32)
            total = total * norm
            ref[:, 512 * half:512 * half + 512] = jnp.where(c == 0, total[:8], total[8:])
    for at in range(4):
        out_copy(at).wait()
    dhid_out.wait()
    gf_out.wait()


def hand_over(*refs):
    count = 6
    sources, targets, held = refs[:count], refs[count:2 * count], refs[2 * count:3 * count]
    in_sems, out_sems = refs[3 * count:]
    pieces = [(1, part(at, 256)) for at in range(4)] + [
        (n, slice(None)) for n in (5, 0, 3, 2, 4)
    ]
    reads = [
        pltpu.make_async_copy(sources[n].at[rows], held[n].at[rows], in_sems.at[i])
        for i, (n, rows) in enumerate(pieces)
    ]
    writes = [
        pltpu.make_async_copy(held[n].at[rows], targets[n].at[rows], out_sems.at[i])
        for i, (n, rows) in enumerate(pieces)
    ]
    for read in reads:
        read.start()
    for read, write in zip(reads, writes):
        read.wait()
        write.start()
    for write in writes:
        write.wait()


def on_device(
    hidden, grid_emb, targets, area_w, field_w, edge_table, halo_rows,
    w_query, w_keyval, w_attn_out, w_fields,
):
    def vm(*shape, dtype=BF16):
        return pltpu.VMEM(shape, dtype)

    def sems(*shape):
        return pltpu.SemaphoreType.DMA(shape)

    def comm(lead, count):
        return [
            vm(*lead, 2, 2, count, 256, 256), vm(*lead, 2, count, 256, 256),
            vm(*lead, 2, 3, count, 64, 256), vm(*lead, 2, count, 64, 256),
            vm(*lead, 2, 3, count, 16, 256), vm(*lead, count, 16, 512),
        ]

    square = (1024, 1024)
    scratch = [
        vm(100, 1024, dtype=F32), vm(100, 1024), vm(128, 1024), vm(100, 1024, dtype=F32),
        vm(*square), vm(*square), vm(2048, 1024), vm(*square), vm(*square),
        vm(*square), vm(*square), vm(*square), vm(*square),
        vm(256, 1024), vm(2048, 256), vm(3, 256, 1024), vm(3, 2048, 1024),
        vm(16, 8, 1024, dtype=F32),
        vm(128, 1024), vm(1024, 128), vm(8, 128, dtype=F32), vm(128, 128, dtype=F32),
        vm(128, 1024, dtype=F32), vm(2, 128, TILE, dtype=F32), vm(2, 8, 16, TILE, dtype=F32),
        vm(2, 8, 16, TILE), vm(128, 1024),
        vm(256, TILE, dtype=F32), vm(4, 256, 512, dtype=F32), vm(128, 1024), vm(*square), vm(*square),
        vm(128, 1024), vm(256, 2048), vm(1024, 256), vm(1024, 256), vm(15, 2, 16, 256),
        vm(8, FIELD_ROWS, 128), vm(8, FIELD_ROWS, 128), vm(4, FIELD_ROWS, 128),
        vm(4, FIELD_ROWS, 128), vm(8, FIELD_ROWS, 128),
        *comm((), 4), *comm((4,), 1),
        vm(2, 1, 256, 512), vm(2, 3, 1, 64, 512), vm(2, 1, 64, 512), vm(2, 3, 1, 16, 512),
        vm(2, 8, 16, 512),
        sems(8), sems(4), sems(4), sems(7), sems(8), sems(2, 8), sems(2, 8), sems(2, 8),
        sems(2, 8), sems(4), sems(4), sems(4, 2), sems(8), sems(4, 2, 4), sems(8, 4),
        sems(15), sems(15),
        sems(8), sems(8), sems(4), sems(4), sems(4), sems(4), sems(8), sems(8),
        sems(5), sems(5), sems(6, 2, 3), sems(6, 2, 3), sems(6, 2, 3), sems(6, 2, 3),
        sems(5, 8), sems(2, 8), sems(6),
    ]
    vmem = pl.BlockSpec(memory_space=pltpu.VMEM)
    hbm = pl.BlockSpec(memory_space=pl.ANY)
    shapes = (
        jax.ShapeDtypeStruct((128, 1024), BF16),
        jax.ShapeDtypeStruct(square, BF16),
        jax.ShapeDtypeStruct((8, 1024), F32),
        jax.ShapeDtypeStruct((16, 1024), F32),
        jax.ShapeDtypeStruct((8, 1024), F32),
        jax.ShapeDtypeStruct((100, 1024), F32),
    )
    raw = pl.pallas_call(
        kernel,
        out_shape=shapes,
        in_specs=[hbm, hbm, hbm, vmem, vmem, vmem, vmem, hbm, hbm, hbm, hbm],
        out_specs=(hbm, hbm, vmem, vmem, vmem, hbm),
        scratch_shapes=scratch,
        compiler_params=pltpu.CompilerParams(
            collective_id=0, has_side_effects=True, vmem_limit_bytes=63 * 1024 * 1024
        ),
        cost_estimate=pl.CostEstimate(
            flops=22_000_000_000, bytes_accessed=16_000_000, transcendentals=500_000
        ),
        name="decoder_backward",
    )(
        hidden[0], grid_emb[0], targets, area_w.reshape(1, 1024), field_w.reshape(1, 100),
        edge_table.T, halo_rows, w_query, w_keyval, w_attn_out, w_fields,
    )
    outs = pl.pallas_call(
        hand_over,
        out_shape=shapes,
        in_specs=[hbm] * 6,
        out_specs=(hbm,) * 6,
        scratch_shapes=[pltpu.VMEM(shape.shape, shape.dtype) for shape in shapes]
        + [sems(9), sems(9)],
        compiler_params=pltpu.CompilerParams(vmem_limit_bytes=63 * 1024 * 1024),
        cost_estimate=pl.CostEstimate(flops=0, bytes_accessed=6_000_000, transcendentals=0),
        name="hand_over",
    )(*raw)
    return (outs[0][None], outs[1][None], *outs[2:])


def solution(mesh):
    in_specs = (
        P("member", "mp", None),
        P("member", "mp", None),
        P(None, "mp"),
        P("mp"),
        P(),
        P("mp", None),
        P("mp", None),
        P(),
        P(),
        P(),
        P(),
    )
    out_specs = (
        P("member", "mp", None),
        P("member", "mp", None),
        P(("member", "mp"), None),
        P(("member", "mp"), None),
        P(("member", "mp"), None),
        P(),
    )
    return jax.shard_map(
        on_device, mesh=mesh, in_specs=in_specs, out_specs=out_specs, check_vma=False
    )
```

```python
import math

import jax
import jax.numpy as jnp
from jax import lax
from jax.experimental import pallas as pl
from jax.experimental.pallas import tpu as pltpu
from jax.sharding import PartitionSpec as P

ALPHA_FAIR = 0.95
KAPPA = 0.1
OFFSETS = (-2, -1, 1, 2)
MEMBERS = 8
FIELD_ROWS = 112
TILE = 512
MESH = pl.DeviceIdType.MESH
BF16 = jnp.bfloat16
F32 = jnp.float32
NT = (((1,), (1,)), ((), ()))
NN = (((1,), (0,)), ((), ()))


def dot(left, right, numbers=NN):
    return lax.dot_general(left, right, numbers, preferred_element_type=F32)


def soft_sign(value):
    return value * lax.rsqrt(value * value + KAPPA * KAPPA)


def blocks(count, body, unroll=1):
    def step(at, carry):
        body(at)
        return carry

    lax.fori_loop(0, count, step, 0, unroll=unroll)


def part(at, size, base=0):
    return pl.ds(pl.multiple_of(base + at * size, size), size)


def kernel(
    hid_hbm, grid_hbm, tgt_hbm, area_ref, field_ref, edge_ref, halo_ref,
    wq_hbm, wkv_hbm, wo_hbm, wf_hbm,
    dhid_hbm, dgrid_hbm, gq_ref, gkv_ref, go_ref, gf_hbm,
    tgt_ref, wf_ref, dhid_ref, gf_ref,
    grid_v, wq_v, wkv_v, wo_v, wot_v, tgrid, qt, att, mix, th, tkv, oh, kvg, wts,
    wfp, wft, frow, fcol, tpad, preds, predr, dps, dpf,
    datt, dpart, outgo, hall, dq,
    drecv, dkfull, kvr, kvh, direct,
    fs, fr1, fr2, fr3, fr4,
    w_g, w_recv, w_r1, w_s1, w_r2, w_fin,
    h_g, h_recv, h_r1, h_s1, h_r2, h_fin,
    k_own, k_r1, k_s1, k_r2,
    rx,
    load_sem, halo_s, halo_r, all_s, all_r, ps_s, ps_r, dp_s, dp_r, back_s, back_r, kv_s, kv_r,
    kvh_s, kvh_r, direct_s, direct_r,
    f1_s, f1_r, f2_s, f2_r, f3_s, f3_r, f4_s, f4_r,
    core_s, core_r, one_s, one_r, two_s, two_r, x_s, x_r, out_sem,
):
    me = lax.axis_index("member")
    mp = lax.axis_index("mp")
    x, c = lax.div(me, 2), lax.rem(me, 2)
    y, z = lax.div(mp, 4), lax.rem(mp, 4)
    other = 1 - c
    sibling = (2 * x + other, mp)
    norm = 1.0 / math.sqrt(MEMBERS * 16384.0)

    def halo_peer(by):
        return (me, lax.rem(mp + by + 16, 16))

    def member_peer(by):
        return lax.rem(me + by, 8)

    def x_peer(by):
        return 2 * lax.rem(x + by, 4) + c

    def y_peer(by):
        return (me, 4 * lax.rem(y + by, 4) + z)

    def z_peer(by):
        return (me, 4 * y + lax.rem(z + by, 4))

    def remote(src, dst, send, recv, device):
        return pltpu.make_async_remote_copy(
            src_ref=src, dst_ref=dst, send_sem=send, recv_sem=recv,
            device_id=device, device_id_type=MESH,
        )

    loads = [
        pltpu.make_async_copy(src, dst, load_sem.at[n])
        for n, (src, dst) in enumerate((
            (hid_hbm, th.at[pl.ds(0, 128)]), (grid_hbm, grid_v), (wq_hbm, wq_v),
            (wkv_hbm, wkv_v), (wo_hbm, wo_v), (hid_hbm, hall.at[part(me, 128)]),
            (tgt_hbm, tgt_ref), (wf_hbm, wf_ref),
        ))
    ]
    for load in loads:
        load.start()
    barrier = pltpu.get_barrier_semaphore()
    partners = (
        [halo_peer(by) for by in OFFSETS]
        + [(member_peer(by), mp) for by in range(1, 8)]
        + [y_peer(by) for by in range(1, 4)]
    )
    for partner in partners:
        pl.semaphore_signal(barrier, inc=1, device_id=partner, device_id_type=MESH)

    for e in range(3):
        oh[e] = (
            lax.broadcasted_iota(jnp.int32, (256, 1024), 0) == edge_ref[e:e + 1, :]
        ).astype(BF16)
    loads[7].wait()
    wfp[...] = jnp.zeros_like(wfp)
    wfp[pl.ds(0, 100), :] = wf_ref[...]
    wft[...] = wfp[...].T
    frow[...] = jnp.zeros_like(frow)
    frow[pl.ds(0, 1), pl.ds(0, 100)] = field_ref[...]
    fcol[...] = jnp.broadcast_to(frow[pl.ds(0, 1), :], (128, 128)).T

    halo_row = jnp.concatenate([halo_ref[l:l + 1, :] for l in range(4)], axis=1)
    halo_home = (
        lax.broadcasted_iota(jnp.int32, (128, 128), 0) == halo_row
    ).astype(BF16)
    loads[0].wait()
    outgo[...] = dot(halo_home.T, th[pl.ds(0, 128), :]).astype(BF16)
    pl.semaphore_wait(barrier, len(partners))
    halos = []
    for l, by in enumerate(OFFSETS):
        copy = remote(
            outgo.at[pl.ds(32 * l, 32)], th.at[pl.ds(128 + 32 * (3 - l), 32)],
            halo_s.at[l], halo_r.at[3 - l], halo_peer(by),
        )
        copy.start()
        halos.append(copy)

    def share(source, at, device):
        return remote(
            hall.at[part(source, 128)] if at > 3 else th.at[pl.ds(0, 128)],
            hall.at[part(source, 128)], all_s.at[at], all_r.at[source], device,
        )

    for by in (1, 3, 2):
        share(me, by, (x_peer(by), mp)).start()
    share(me, 0, sibling).start()

    loads[1].wait()

    def turn(at):
        tgrid[:, part(at, 256)] = grid_v[part(at, 256), :].T
    blocks(4, turn)
    loads[2].wait()
    for at in range(2):
        lanes = pl.ds(TILE * at, TILE)
        qt[:, lanes] = dot(wq_v[...], tgrid[:, lanes]).astype(BF16)

    def make_table(first):
        rows = pl.ds(first, 128)

        def rows_of(at):
            tkv[part(at, 512), rows] = dot(wkv_v[part(at, 512), :], th[rows, :], NT).astype(BF16)
        blocks(4, rows_of)

    loads[3].wait()
    make_table(0)
    loads[4].wait()

    def turn_out(at):
        wot_v[:, part(at, 256)] = wo_v[part(at, 256), :].T
    blocks(4, turn_out)
    for copy in halos:
        copy.wait()
    make_table(128)
    loads[6].wait()
    tpad[...] = jnp.zeros_like(tpad)
    tpad[pl.ds(0, 100), :] = tgt_ref[...]

    def gather(t):
        lanes = pl.ds(t * TILE, TILE)
        for e in range(3):
            def rows_of(at, e=e):
                kvg[e, part(at, 512), lanes] = dot(
                    tkv[part(at, 512), :], oh[e, :, lanes]
                ).astype(BF16)
            blocks(4, rows_of)

    def attend(t):
        lanes = pl.ds(t * TILE, TILE)

        def head(h):
            rows, vrows = part(h, 64), part(h, 64, 1024)
            query = qt[rows, lanes].astype(F32)
            raised = []
            for e in range(3):
                key = kvg[e, rows, lanes].astype(F32)
                raised.append(jnp.exp(jnp.sum(query * key, axis=0, keepdims=True) * 0.125))
            total = raised[0] + raised[1] + raised[2]
            out = None
            for e in range(3):
                weight = raised[e] / total
                wts[h, e:e + 1, lanes] = weight
                term = weight.astype(BF16).astype(F32) * kvg[e, vrows, lanes].astype(F32)
                out = term if out is None else out + term
            att[rows, lanes] = out.astype(BF16)
        blocks(16, head, 2)

    def pred_copy(t, by):
        target = member_peer(by)
        return remote(
            preds.at[t, part(target, 16)], predr.at[t, me], ps_s.at[t, by], ps_r.at[t, me],
            (target, mp),
        )

    def predict(t):
        lanes = pl.ds(t * TILE, TILE)
        mixed = (tgrid[:, lanes].astype(F32) + dot(wo_v[...], att[:, lanes])).astype(BF16)
        mix[:, lanes] = mixed
        preds[t] = dot(wfp[...], mixed)
        for by in range(1, 8):
            pred_copy(t, by).start()
        predr[t, me] = preds[t, part(me, 16), :]

    fair = (1.0 - (1.0 - ALPHA_FAIR) / MEMBERS) / (MEMBERS * (MEMBERS - 1))
    mine = part(me, 16)

    def dp_copy(t, by):
        target = member_peer(by)
        return remote(
            dps.at[t, target], dpf.at[mine, pl.ds(t * TILE, TILE)],
            dp_s.at[t, by], dp_r.at[t, me], (target, mp),
        )

    def crps(t):
        for by in range(1, 8):
            source = member_peer(by)
            remote(preds.at[t, part(source, 16)], predr.at[t, source], ps_s.at[t, by],
                   ps_r.at[t, source], (source, mp)).wait_recv()
            pred_copy(t, by).wait_send()
        for chunk in range(TILE // 128):
            lanes = pl.ds(128 * chunk, 128)
            points = pl.ds(t * TILE + 128 * chunk, 128)
            truth = tpad[mine, points]
            scale = fcol[mine, :] * area_ref[:, points]
            pred = [predr[t, m, :, lanes] for m in range(MEMBERS)]
            spread = [jnp.zeros((16, 128), F32) for _ in range(MEMBERS)]
            for i in range(MEMBERS):
                for j in range(i + 1, MEMBERS):
                    term = soft_sign(pred[i] - pred[j])
                    spread[i] = spread[i] + term
                    spread[j] = spread[j] - term
            for m in range(MEMBERS):
                dps[t, m, :, lanes] = (
                    scale * (soft_sign(pred[m] - truth) * (1.0 / MEMBERS) - fair * spread[m])
                ).astype(BF16)
        for by in range(1, 8):
            dp_copy(t, by).start()
        dpf[mine, pl.ds(t * TILE, TILE)] = dps[t, me]

    dmix = tgrid

    def make_dmix(t):
        lanes = pl.ds(t * TILE, TILE)
        for by in range(1, 8):
            source = member_peer(by)
            remote(dps.at[t, source], dpf.at[part(source, 16), lanes], dp_s.at[t, by],
                   dp_r.at[t, source], (source, mp)).wait_recv()
            dp_copy(t, by).wait_send()

        def rows_of(at):
            dmix[part(at, 512), lanes] = dot(wft[part(at, 512), :], dpf[:, lanes]).astype(BF16)
        blocks(2, rows_of)

    gather(0)
    attend(0)
    predict(0)
    gather(1)
    attend(1)
    crps(0)
    predict(1)

    for by in range(1, 4):
        source = x_peer(by)
        share(me, by, (x_peer(by), mp)).wait_send()
        share(source, 0, sibling).wait_recv()
        share(source, 3 + by, sibling).start()
    share(me, 0, sibling).wait_send()

    dkv = [
        wo_v.at[pl.ds(512 * (e // 2), 512), pl.ds(512 * (e % 2), 512)] for e in range(3)
    ]

    def block_of(n):
        return lax.rem(x + n, 4)

    def attend_back(n, t):
        j = block_of(n)
        base = pl.multiple_of(j * 256, 256)
        lanes = pl.ds(t * TILE, TILE)
        datt[...] = dot(wot_v[pl.ds(base, 256), :], dmix[:, lanes])

        def head(hh):
            local, vlocal = part(hh, 64), part(hh, 64, 256)
            rows = pl.ds(pl.multiple_of(base + hh * 64, 64), 64)
            vrows = pl.ds(pl.multiple_of(1024 + base + hh * 64, 64), 64)
            grad = datt[local, :]
            query = qt[rows, lanes].astype(F32)
            weight = [wts[4 * j + hh, e:e + 1, lanes] for e in range(3)]
            d_weight = [
                jnp.sum(grad * kvg[e, vrows, lanes].astype(F32), axis=0, keepdims=True)
                for e in range(3)
            ]
            inner = weight[0] * d_weight[0] + weight[1] * d_weight[1] + weight[2] * d_weight[2]
            out = None
            for e in range(3):
                d_score = weight[e] * (d_weight[e] - inner) * 0.125
                term = d_score * kvg[e, rows, lanes].astype(F32)
                out = term if out is None else out + term
                dkv[e][local, :] = (d_score * query).astype(BF16)
                dkv[e][vlocal, :] = (weight[e].astype(BF16).astype(F32) * grad).astype(BF16)
            dq[rows, lanes] = out.astype(BF16)
        blocks(4, head)
        total = dot(oh[0, :, lanes], dkv[0][...], NT)
        for e in range(1, 3):
            total = total + dot(oh[e, :, lanes], dkv[e][...], NT)
        if t == 0:
            dpart[n - 1] = total
        else:
            send_keyval(n, total + dpart[n - 1])

    def kv_targets(n):
        j = block_of(n)
        return (j, 4 + j)

    def kv_copy(n, which):
        target = kv_targets(n)[which]
        return remote(
            dkfull.at[pl.ds(0, 128), part(target, 256)], kvr.at[part(me, 128)],
            kv_s.at[n - 1, which], kv_r.at[me], (target, mp),
        )

    def kvh_copy(n, which, r):
        target = kv_targets(n)[which]
        return remote(
            dkfull.at[pl.ds(128 + 32 * r, 32), part(target, 256)],
            kvh.at[pl.ds(pl.multiple_of(me * 128 + 32 * (3 - r), 32), 32)],
            kvh_s.at[n - 1, which, r], kvh_r.at[me, 3 - r],
            (target, halo_peer(OFFSETS[r])[1]),
        )

    def send_keyval(n, total):
        for which in range(2):
            target = kv_targets(n)[which]
            piece = total[:, 256 * which:256 * which + 256].astype(BF16)
            dkfull[:, part(target, 256)] = piece

            @pl.when(target != me)
            def _():
                kv_copy(n, which).start()

            @pl.when(target == me)
            def _():
                kvr[part(me, 128), :] = piece[:128]

            for r in range(4):
                kvh_copy(n, which, r).start()

    def wait_keyval():
        for by in range(1, 8):
            source = member_peer(by)
            remote(kvr.at[part(source, 128)], kvr.at[part(source, 128)], kv_s.at[0, 0],
                   kv_r.at[source], (source, mp)).wait_recv()
        for source in range(MEMBERS):
            for r in range(4):
                rows = pl.ds(source * 128 + 32 * r, 32)
                remote(kvh.at[rows], kvh.at[rows], kvh_s.at[0, 0, r], kvh_r.at[source, r],
                       halo_peer(OFFSETS[r])).wait_recv()

    def end_keyval():
        for n in range(1, 5):
            for which in range(2):
                @pl.when(kv_targets(n)[which] != me)
                def _():
                    kv_copy(n, which).wait_send()

                for r in range(4):
                    kvh_copy(n, which, r).wait_send()

    def ring(half, by):
        return y_peer(by) if half == 0 else z_peer(by)

    def store_unit(ref, unit, value, crossed=True):
        for core in range(2):
            for half in range(2):
                at = 512 * core + 256 * half
                piece = value[:, at:at + 256].reshape(2, 4, 4, 8, 256)
                order = (2, 1, 0, 3, 4) if half == 1 and crossed else (1, 2, 0, 3, 4)
                piece = piece.transpose(order).reshape(256, 256)
                ref[core, half, unit] = piece.astype(BF16)

    units = [4, 1, 1, 1, 1, 1]
    sets = [(w_g, w_recv, w_g.at[c], w_r1, w_s1, w_r2, w_fin)] + [
        (h_g.at[n], h_recv.at[n], h_g.at[n, c], h_r1.at[n], h_s1.at[n], h_r2.at[n], h_fin.at[n])
        for n in range(4)
    ] + [(None, None, k_own, k_r1, k_s1, k_r2, None)]

    def core_copy(n):
        return remote(sets[n][0].at[other], sets[n][1], core_s.at[n], core_r.at[n], sibling)

    def one_copy(n, half, by):
        first = lax.rem((y if half == 0 else z) + by, 4)
        return remote(
            sets[n][2].at[half, :, part(first, 64), :], sets[n][3].at[half, by - 1],
            one_s.at[n, half, by - 1], one_r.at[n, half, by - 1], ring(half, by),
        )

    def two_copy(n, half, by):
        second = lax.rem((z if half == 0 else y) + by, 4)
        return remote(
            sets[n][4].at[half, :, part(second, 16), :], sets[n][5].at[half, by - 1],
            two_s.at[n, half, by - 1], two_r.at[n, half, by - 1], ring(1 - half, by),
        )

    def add_cores(n, half):
        own, recv = sets[n][2], sets[n][1]

        def add(unit):
            own[half, unit] = (
                own[half, unit].astype(F32) + recv[half, unit].astype(F32)
            ).astype(BF16)
        blocks(units[n], add)

    def start_one(n):
        core_copy(n).wait()
        for half in range(2):
            add_cores(n, half)
            for by in (2, 1, 3):
                one_copy(n, half, by).start()

    def direct_copy(by):
        target = lax.rem(mp + by, 16)
        return remote(
            sets[4][2].at[:, 0, part(target, 16), :], direct.at[by - 1],
            direct_s.at[by - 1], direct_r.at[by - 1], (me, target),
        )

    def start_direct():
        core_copy(4).wait()
        for half in range(2):
            add_cores(4, half)
        for by in (10, 6, 9, 7, 8, 5, 11, 2, 14, 3, 13, 1, 15, 4, 12):
            direct_copy(by).start()

    def end_direct():
        for by in range(1, 16):
            direct_copy(by).wait()
        for half in range(2):
            total = sets[4][2][half, 0, part(mp, 16), :].astype(F32)
            for by in range(1, 16):
                total = total + direct[by - 1, half].astype(F32)
            sets[4][6][0, :, 256 * half:256 * half + 256] = total.astype(BF16)
        send_x(4)

    def start_two(n):
        own, r1, s1 = sets[n][2], sets[n][3], sets[n][4]
        for half in range(2):
            for by in (1, 3, 2):
                one_copy(n, half, by).wait()
            first = part(y if half == 0 else z, 64)
            for unit in range(units[n]):
                total = own[half, unit, first, :].astype(F32)
                for slot in range(3):
                    total = total + r1[half, slot, unit].astype(F32)
                s1[half, unit] = total.astype(BF16)
            for by in (2, 1, 3):
                two_copy(n, half, by).start()

    def finish_two(n, half, unit):
        total = sets[n][4][half, unit, part(z if half == 0 else y, 16), :].astype(F32)
        for slot in range(3):
            total = total + sets[n][5][half, slot, unit].astype(F32)
        return total

    def x_targets(n):
        if n == 0:
            return [(0, i, 2 * i + k) for i in range(4) for k in range(2)]
        j = block_of(n)
        return [(1, 0, 2 * j), (1, 0, 2 * j + 1)]

    def x_copy(n, index, kind, unit, target):
        return remote(
            sets[n][6].at[unit], rx.at[kind, me], x_s.at[n, index], x_r.at[kind, me],
            (target, mp),
        )

    def start_x(n):
        fin = sets[n][6]
        for half in range(2):
            for by in (1, 3, 2):
                two_copy(n, half, by).wait()
            for unit in range(units[n]):
                fin[unit, :, 256 * half:256 * half + 256] = finish_two(n, half, unit).astype(BF16)
        send_x(n)

    def send_x(n):
        fin = sets[n][6]
        for index, (kind, unit, target) in enumerate(x_targets(n)):
            @pl.when(target != me)
            def _():
                x_copy(n, index, kind, unit, target).start()

            @pl.when(target == me)
            def _():
                rx[kind, me] = fin[unit]

    def end_x(n):
        for index, (kind, unit, target) in enumerate(x_targets(n)):
            @pl.when(target != me)
            def _():
                x_copy(n, index, kind, unit, target).wait_send()

    def query_grad(n):
        span = part(block_of(n), 256)
        store_unit(sets[n][0], 0, dot(dq[span, :], grid_v[...]), n < 4)
        core_copy(n).start()

    def out_grad():
        for at in range(2):
            value = dot(dmix[pl.ds(512 * at, 512), :], att[...], NT)
            for k in range(2):
                store_unit(w_g, 2 * at + k, value[256 * k:256 * k + 256])
        core_copy(0).start()

    def fields_grad():
        value = dot(dpf[pl.ds(0, FIELD_ROWS), :], mix[...], NT)
        for j in range(MEMBERS):
            fs[j] = value[:, 128 * j:128 * j + 128].astype(BF16)
        for by in range(1, 8):
            f1_copy(by).start()
        fr1[me] = fs[me]

    def f1_copy(by):
        target = member_peer(by)
        return remote(fs.at[target], fr1.at[me], f1_s.at[by], f1_r.at[me], (target, mp))

    def f2_copy(by):
        return remote(fr2.at[y], fr2.at[y], f2_s.at[by], f2_r.at[y], y_peer(by))

    def f3_copy(by):
        return remote(fr3.at[z], fr3.at[z], f3_s.at[by], f3_r.at[z], z_peer(by))

    def f4_copy(by):
        return remote(fr4.at[me], fr4.at[me], f4_s.at[by], f4_r.at[me], (member_peer(by), mp))

    def slots_sum(ref, count):
        total = ref[0].astype(F32)
        for slot in range(1, count):
            total = total + ref[slot].astype(F32)
        return total

    def start_f2():
        for by in range(1, 8):
            source = member_peer(by)
            remote(fs.at[source], fr1.at[source], f1_s.at[by], f1_r.at[source],
                   (source, mp)).wait_recv()
            f1_copy(by).wait_send()
        fr2[y] = slots_sum(fr1, 8).astype(BF16)
        for by in range(1, 4):
            f2_copy(by).start()

    def start_f3():
        for by in range(1, 4):
            source = lax.rem(y + by, 4)
            remote(fr2.at[source], fr2.at[source], f2_s.at[by], f2_r.at[source],
                   y_peer(by)).wait_recv()
            f2_copy(by).wait_send()
        fr3[z] = slots_sum(fr2, 4).astype(BF16)
        for by in range(1, 4):
            f3_copy(by).start()

    def start_f4():
        for by in range(1, 4):
            source = lax.rem(z + by, 4)
            remote(fr3.at[source], fr3.at[source], f3_s.at[by], f3_r.at[source],
                   z_peer(by)).wait_recv()
            f3_copy(by).wait_send()
        fr4[me] = (slots_sum(fr3, 4) * norm).astype(BF16)
        for by in range(1, 8):
            f4_copy(by).start()

    def end_f4():
        for by in range(1, 8):
            source = member_peer(by)
            remote(fr4.at[source], fr4.at[source], f4_s.at[by], f4_r.at[source],
                   (source, mp)).wait_recv()
            f4_copy(by).wait_send()
        for j in range(MEMBERS):
            gf_ref[:, 128 * j:128 * j + 128] = fr4[j, pl.ds(0, 100), :].astype(F32)

    make_dmix(0)
    attend_back(1, 0)
    crps(1)
    attend_back(2, 0)
    attend_back(3, 0)
    attend_back(4, 0)
    make_dmix(1)
    out_grad()
    fields_grad()
    attend_back(1, 1)
    start_one(0)
    query_grad(1)
    attend_back(2, 1)
    query_grad(2)
    start_one(1)
    attend_back(3, 1)
    query_grad(3)
    start_f2()
    start_one(2)
    attend_back(4, 1)
    query_grad(4)
    start_one(3)

    def back_copy(r):
        return remote(
            outgo.at[pl.ds(32 * r, 32)], drecv.at[pl.ds(32 * (3 - r), 32)],
            back_s.at[r], back_r.at[3 - r], halo_peer(OFFSETS[r]),
        )

    through_kv = dot(dkfull[...], wkv_v[...])
    outgo[...] = through_kv[128:].astype(BF16)
    own_hidden = through_kv[:128]
    for r in range(4):
        back_copy(r).start()
    start_direct()

    stage = att

    def out_copy(at):
        return pltpu.make_async_copy(
            stage.at[part(at, 256)], dgrid_hbm.at[part(at, 256)], out_sem.at[at]
        )

    def grid_grad(at):
        span = pl.ds(256 * at, 256)
        through = dot(dq[:, span].T, wq_v[...])
        direct = dot(dpf[:, span].T, wfp[...]).astype(BF16).astype(F32)
        stage[span, :] = (direct + through).astype(BF16)
        out_copy(at).start()

    grid_grad(0)
    start_two(0)
    start_two(1)
    grid_grad(1)
    start_f3()
    start_two(2)
    start_two(3)
    grid_grad(2)
    start_x(0)
    start_x(1)

    loads[5].wait()
    for by in range(4):
        source = 2 * lax.rem(x + by, 4) + other
        share(source, 0, sibling).wait_recv()
    wait_keyval()
    for m in range(MEMBERS):
        rows = pl.ds(128 * m, 128)
        kvr[rows, :] = (
            kvr[rows, :].astype(F32) + dot(halo_home, kvh[rows, :])
        ).astype(BF16)
    value = dot(kvr[...].T, hall[...])
    k_own[0, 0] = value[:, :512].astype(BF16)
    k_own[1, 0] = (
        value[:, 512:].reshape(4, 4, 16, 512).transpose(1, 0, 2, 3).reshape(256, 512)
    ).astype(BF16)
    for half in range(2):
        for by in (2, 1, 3):
            one_copy(5, half, by).start()

    for r in range(4):
        back_copy(r).wait()
    dhid_ref[...] = (own_hidden + dot(halo_home, drecv[...])).astype(BF16)
    dhid_out = pltpu.make_async_copy(dhid_ref, dhid_hbm, out_sem.at[4])
    dhid_out.start()
    start_f4()
    grid_grad(3)
    start_two(5)
    start_x(2)
    start_x(3)
    end_direct()
    end_f4()
    gf_out = pltpu.make_async_copy(gf_ref, gf_hbm, out_sem.at[5])
    gf_out.start()
    end_keyval()
    for half in range(2):
        for by in (1, 3, 2):
            two_copy(5, half, by).wait()
        gkv_ref[:, 512 * half:512 * half + 512] = finish_two(5, half, 0) * norm
    for n in range(5):
        end_x(n)
    for by in range(1, 4):
        share(x_peer(by), 3 + by, sibling).wait_send()
    for kind in range(2):
        for by in range(1, 8):
            source = member_peer(by)
            remote(rx.at[kind, source], rx.at[kind, source], x_s.at[0, 0],
                   x_r.at[kind, source], (source, mp)).wait_recv()
    for kind, ref in ((0, go_ref), (1, gq_ref)):
        for half in range(2):
            total = rx[kind, half].astype(F32)
            for by in range(1, 4):
                total = total + rx[kind, 2 * by + half].astype(F32)
            total = total * norm
            ref[:, 512 * half:512 * half + 512] = jnp.where(c == 0, total[:8], total[8:])
    for at in range(4):
        out_copy(at).wait()
    dhid_out.wait()
    gf_out.wait()


def hand_over(*refs):
    count = 6
    sources, targets, held = refs[:count], refs[count:2 * count], refs[2 * count:3 * count]
    in_sems, out_sems = refs[3 * count:]
    pieces = [(1, part(at, 256)) for at in range(4)] + [
        (n, slice(None)) for n in (5, 0, 3, 2, 4)
    ]
    reads = [
        pltpu.make_async_copy(sources[n].at[rows], held[n].at[rows], in_sems.at[i])
        for i, (n, rows) in enumerate(pieces)
    ]
    writes = [
        pltpu.make_async_copy(held[n].at[rows], targets[n].at[rows], out_sems.at[i])
        for i, (n, rows) in enumerate(pieces)
    ]
    for read in reads:
        read.start()
    for read, write in zip(reads, writes):
        read.wait()
        write.start()
    for write in writes:
        write.wait()


def on_device(
    hidden, grid_emb, targets, area_w, field_w, edge_table, halo_rows,
    w_query, w_keyval, w_attn_out, w_fields,
):
    def vm(*shape, dtype=BF16):
        return pltpu.VMEM(shape, dtype)

    def sems(*shape):
        return pltpu.SemaphoreType.DMA(shape)

    def comm(lead, count):
        return [
            vm(*lead, 2, 2, count, 256, 256), vm(*lead, 2, count, 256, 256),
            vm(*lead, 2, 3, count, 64, 256), vm(*lead, 2, count, 64, 256),
            vm(*lead, 2, 3, count, 16, 256), vm(*lead, count, 16, 512),
        ]

    square = (1024, 1024)
    scratch = [
        vm(100, 1024, dtype=F32), vm(100, 1024), vm(128, 1024), vm(100, 1024, dtype=F32),
        vm(*square), vm(*square), vm(2048, 1024), vm(*square), vm(*square),
        vm(*square), vm(*square), vm(*square), vm(*square),
        vm(256, 1024), vm(2048, 256), vm(3, 256, 1024), vm(3, 2048, 1024),
        vm(16, 8, 1024, dtype=F32),
        vm(128, 1024), vm(1024, 128), vm(8, 128, dtype=F32), vm(128, 128, dtype=F32),
        vm(128, 1024, dtype=F32), vm(2, 128, TILE, dtype=F32), vm(2, 8, 16, TILE, dtype=F32),
        vm(2, 8, 16, TILE), vm(128, 1024),
        vm(256, TILE, dtype=F32), vm(4, 256, 512, dtype=F32), vm(128, 1024), vm(*square), vm(*square),
        vm(128, 1024), vm(256, 2048), vm(1024, 256), vm(1024, 256), vm(15, 2, 16, 256),
        vm(8, FIELD_ROWS, 128), vm(8, FIELD_ROWS, 128), vm(4, FIELD_ROWS, 128),
        vm(4, FIELD_ROWS, 128), vm(8, FIELD_ROWS, 128),
        *comm((), 4), *comm((4,), 1),
        vm(2, 1, 256, 512), vm(2, 3, 1, 64, 512), vm(2, 1, 64, 512), vm(2, 3, 1, 16, 512),
        vm(2, 8, 16, 512),
        sems(8), sems(4), sems(4), sems(7), sems(8), sems(2, 8), sems(2, 8), sems(2, 8),
        sems(2, 8), sems(4), sems(4), sems(4, 2), sems(8), sems(4, 2, 4), sems(8, 4),
        sems(15), sems(15),
        sems(8), sems(8), sems(4), sems(4), sems(4), sems(4), sems(8), sems(8),
        sems(5), sems(5), sems(6, 2, 3), sems(6, 2, 3), sems(6, 2, 3), sems(6, 2, 3),
        sems(5, 8), sems(2, 8), sems(6),
    ]
    vmem = pl.BlockSpec(memory_space=pltpu.VMEM)
    hbm = pl.BlockSpec(memory_space=pl.ANY)
    shapes = (
        jax.ShapeDtypeStruct((128, 1024), BF16),
        jax.ShapeDtypeStruct(square, BF16),
        jax.ShapeDtypeStruct((8, 1024), F32),
        jax.ShapeDtypeStruct((16, 1024), F32),
        jax.ShapeDtypeStruct((8, 1024), F32),
        jax.ShapeDtypeStruct((100, 1024), F32),
    )
    raw = pl.pallas_call(
        kernel,
        out_shape=shapes,
        in_specs=[hbm, hbm, hbm, vmem, vmem, vmem, vmem, hbm, hbm, hbm, hbm],
        out_specs=(hbm, hbm, vmem, vmem, vmem, hbm),
        scratch_shapes=scratch,
        compiler_params=pltpu.CompilerParams(
            collective_id=0, has_side_effects=True, vmem_limit_bytes=63 * 1024 * 1024
        ),
        cost_estimate=pl.CostEstimate(
            flops=22_000_000_000, bytes_accessed=16_000_000, transcendentals=500_000
        ),
        name="decoder_backward",
    )(
        hidden[0], grid_emb[0], targets, area_w.reshape(1, 1024), field_w.reshape(1, 100),
        edge_table.T, halo_rows, w_query, w_keyval, w_attn_out, w_fields,
    )
    outs = pl.pallas_call(
        hand_over,
        out_shape=shapes,
        in_specs=[hbm] * 6,
        out_specs=(hbm,) * 6,
        scratch_shapes=[pltpu.VMEM(shape.shape, shape.dtype) for shape in shapes]
        + [sems(9), sems(9)],
        compiler_params=pltpu.CompilerParams(vmem_limit_bytes=63 * 1024 * 1024),
        cost_estimate=pl.CostEstimate(flops=0, bytes_accessed=6_000_000, transcendentals=0),
        name="hand_over",
    )(*raw)
    return (outs[0][None], outs[1][None], *outs[2:])


def solution(mesh):
    in_specs = (
        P("member", "mp", None),
        P("member", "mp", None),
        P(None, "mp"),
        P("mp"),
        P(),
        P("mp", None),
        P("mp", None),
        P(),
        P(),
        P(),
        P(),
    )
    out_specs = (
        P("member", "mp", None),
        P("member", "mp", None),
        P(("member", "mp"), None),
        P(("member", "mp"), None),
        P(("member", "mp"), None),
        P(),
    )
    return jax.shard_map(
        on_device, mesh=mesh, in_specs=in_specs, out_specs=out_specs, check_vma=False
    )
```
